32 devices in a mesh: grp: 16 (over z, x, core), mem: 2 (over y).
Axes of the slice: x: 2, y: 2, z: 4, core: 2. Of those that a mesh axis runs over, the one named last changes fastest.
Arguments:
- queries: bfloat16 [8192, 32, 128], P('grp', 'mem'), may hold values from -16 to 16
- suffix_kv: bfloat16 [8192, 2, 4, 128], P('grp'), may hold values from -8 to 8
- prefix_kv: bfloat16 [128, 2, 128, 4, 128], P('grp'), may hold values from -8 to 8
- out_weight: bfloat16 [4096, 2048], P('mem'), may hold values from -0.09375 to 0.09375
- node_blocks: int32 [42], replicated, may hold values from 1 to 32, 128 in all
- root_of: int32 [8], replicated, may hold values from 0 to 1
- mid_of: int32 [32], replicated, may hold values from 0 to 7
Outputs:
- mixed: bfloat16 [8192, 2048], P(('grp', 'mem'))
The draws below stay inside these ranges and needn't reach their ends.
Inputs may be any that keep to these rules, and one draw needn't show every extreme that they name: `node_blocks`: some node has exactly 32 blocks, and all together have 128.
All inputs are finite; a program needn't handle non-finite values.
Results may differ from the reference program's by a relative error of at most 0.025.
Values may be sent and summed in bfloat16 or wider, within the bound.
No kernel may reach another device: no remote copies, remote signals or barrier semaphores. Data moves between devices by JAX's collectives and lax.ppermute only.
A program may use at most 128 MiB of HBM per device.

```python
import math
import jax
import jax.numpy as jnp
import numpy as np
from jax import lax

D = 2048
QH = 32
KVH = 4
HD = 128
SUFFIX = 256
BLOCK = 128
MOST_BLK = 32
NBLK = 128
REQUESTS = 32
N0 = 2
N1 = 8
NODES = 42
TOKENS = 8192


def draw_queries(key, part):
    base_key = jax.random.fold_in(key, 11)
    sampled = jnp.clip(1.6 * jax.random.normal(base_key, (TOKENS, QH, HD), jnp.float32), -8.0, 8.0)
    return sampled.astype(jnp.bfloat16)


def draw_suffix_kv(key, part):
    base_key = jax.random.fold_in(key, 23)
    sampled = jnp.clip(1.6 * jax.random.normal(base_key, (TOKENS, 2, KVH, HD), jnp.float32), -8.0, 8.0)
    return sampled.astype(jnp.bfloat16)


def plant(entries, rng, smallest, top_value):
    index_at = [jax.random.randint(jax.random.fold_in(rng, axis), (), 0, length) for axis, length in enumerate(entries.shape)]
    main_axis = entries.shape.index(max(entries.shape))
    beside = index_at[:main_axis] + [(index_at[main_axis] + 1) % entries.shape[main_axis]] + index_at[main_axis + 1:]
    return entries.at[tuple(index_at)].set(smallest).at[tuple(beside)].set(top_value)


def levels(own_key, dims, pieces, least, high):
    factor_of, own = 1.0, jax.random.fold_in(own_key, 6)
    for dim, shards_of in pieces:
        steps = jnp.exp(jax.random.uniform(jax.random.fold_in(own, dim), (shards_of,), jnp.float32, least / len(pieces), high / len(pieces)))
        factor_of = factor_of * jnp.repeat(steps, dims[dim] // shards_of).reshape([-1 if axis == dim else 1 for axis in range(len(dims))])
    return factor_of


def profile(number_of, total, bound, slope):
    loads = [(1 << 20) // math.isqrt(grade ** slope) + 1 for grade in range(2, number_of + 1)]
    rest, holding = total - bound - (number_of - 1), [1] * (number_of - 1)
    while rest > 0:
        movable = [i for i in range(number_of - 1) if holding[i] < bound]
        whole, budget = sum([loads[i] for i in movable]), rest
        for i in movable:
            addition = min(bound - holding[i], max(1, budget * loads[i] // whole), rest)
            holding[i] = holding[i] + addition
            rest = rest - addition
    return np.array([bound] + holding)


def ragged(own_key, amount, total, bound, lean):
    if amount == 2:
        one = jax.random.randint(own_key, (), max(1, total - bound), min(bound, total - 1) + 1)
        return jnp.stack([one, total - one])
    lengths = jnp.asarray(profile(amount, total, bound, lean), jnp.int32)
    pairs = (amount - 1) // 2
    giver, taker = lengths[1:1 + 2 * pairs:2], lengths[2:2 + 2 * pairs:2]
    slack = jnp.minimum(giver - 1, bound - taker)
    moved = jax.random.randint(jax.random.fold_in(own_key, 1), (pairs,), 0, 1 << 20) % (slack + 1)
    lengths = lengths.at[1:1 + 2 * pairs:2].set(giver - moved).at[2:2 + 2 * pairs:2].set(taker + moved)
    return lengths[jax.random.permutation(jax.random.fold_in(own_key, 2), amount)]


def noise(own_key, extent, scale, limit, shards=(), kind=jnp.bfloat16):
    entries = scale * jax.random.normal(own_key, extent, jnp.float32)
    if shards:
        entries = entries * levels(own_key, extent, shards, -0.22, 0.18)
    return jnp.clip(entries, -limit, limit).astype(kind)


def setup_inputs(seed: int = 0) -> dict:
    arg_keys = jax.random.split(jax.random.key(seed), 8)
    queries = draw_queries(jax.random.fold_in(arg_keys[7], 71), 0)
    suffix_kv = draw_suffix_kv(jax.random.fold_in(arg_keys[7], 71), 0)
    prefix_kv = noise(arg_keys[2], (NBLK, 2, BLOCK, KVH, HD), 1.6, 8.0, ((0, 16),))
    out_weight = noise(arg_keys[3], (QH * HD, D), (QH * HD) ** -0.5, 0.09375, ((0, 2),))
    node_blocks = ragged(arg_keys[4], NODES, NBLK, MOST_BLK, 2).astype(jnp.int32)
    root_of = plant(jax.random.randint(arg_keys[5], (N1,), 0, N0), jax.random.fold_in(arg_keys[5], 1), 0, N0 - 1).astype(jnp.int32)
    mid_of = plant(jax.random.randint(arg_keys[6], (REQUESTS,), 0, N1), jax.random.fold_in(arg_keys[6], 1), 0, N1 - 1).astype(jnp.int32)
    return dict(queries=queries, suffix_kv=suffix_kv, prefix_kv=prefix_kv, out_weight=out_weight, node_blocks=node_blocks, root_of=root_of, mid_of=mid_of)


NEG = -1.0e30


def reference(queries, suffix_kv, prefix_kv, out_weight, node_blocks, root_of, mid_of):
    firsts = (jnp.cumsum(node_blocks) - node_blocks).astype(jnp.int32)
    slot_ids = jnp.arange(MOST_BLK, dtype=jnp.int32)
    causal = jnp.arange(SUFFIX)[:, None] >= jnp.arange(SUFFIX)[None, :]
    group_size = QH // KVH

    def one_request(request):
        middle = lax.dynamic_index_in_dim(mid_of, request, 0, keepdims=False)
        root_node = lax.dynamic_index_in_dim(root_of, middle, 0, keepdims=False)
        path_nodes = jnp.stack([root_node, N0 + middle, N0 + N1 + request]).astype(jnp.int32)
        starts = firsts[path_nodes]
        counts = node_blocks[path_nodes]
        in_node = slot_ids[None, :] < counts[:, None]
        block_ids = jnp.where(in_node, starts[:, None] + slot_ids[None, :], 0).reshape(-1).astype(jnp.int32)
        blocks = prefix_kv[block_ids]
        key_ok = jnp.repeat(in_node.reshape(-1), BLOCK)
        own_kv = lax.dynamic_slice_in_dim(suffix_kv, request * SUFFIX, SUFFIX, 0)
        own_q = lax.dynamic_slice_in_dim(queries, request * SUFFIX, SUFFIX, 0)
        allowed = jnp.concatenate([jnp.broadcast_to(key_ok[None, :], (SUFFIX, key_ok.shape[0])), causal], axis=1)
        heads_out = []
        for g in range(KVH):
            key_rows = jnp.concatenate([blocks[:, 0, :, g, :].reshape(-1, HD), own_kv[:, 0, g, :]], axis=0).astype(jnp.float32)
            value_rows = jnp.concatenate([blocks[:, 1, :, g, :].reshape(-1, HD), own_kv[:, 1, g, :]], axis=0).astype(jnp.float32)
            query_rows = own_q[:, g * group_size:(g + 1) * group_size, :].astype(jnp.float32)
            scores = jnp.einsum("sph,th->pst", query_rows, key_rows) * (HD ** -0.5)
            scores = jnp.where(allowed[None], scores, NEG)
            weights = jnp.exp(scores - jnp.max(scores, axis=-1, keepdims=True))
            totals = jnp.sum(weights, axis=-1)
            rounded = lax.optimization_barrier(weights.astype(jnp.bfloat16)).astype(jnp.float32)
            summed = jnp.einsum("pst,th->sph", rounded, value_rows)
            heads_out.append(summed / jnp.transpose(totals)[:, :, None])
        attended = jnp.concatenate(heads_out, axis=1).astype(jnp.bfloat16)
        return attended.reshape(SUFFIX, QH * HD)

    attention = lax.map(one_request, jnp.arange(REQUESTS, dtype=jnp.int32)).reshape(TOKENS, QH * HD)
    return jnp.dot(attention, out_weight, preferred_element_type=jnp.float32).astype(jnp.bfloat16)
```

```python
import functools

import jax
import jax.numpy as jnp
from jax import lax
from jax.experimental import pallas as pl
from jax.experimental.pallas import tpu as pltpu
from jax.sharding import PartitionSpec as P

QH = 32
KVH = 4
SUFFIX = 256
CORES = 2
NEG = -1e30
LOG2E = 1.4426950408889634


def path_ranges(request_ids, node_blocks, root_of, mid_of):
    nodes_all = node_blocks.shape[0]
    middles_all = root_of.shape[0]
    leaves = mid_of.shape[0]
    roots_all = nodes_all - middles_all - leaves
    firsts = jnp.cumsum(node_blocks) - node_blocks
    middles = jnp.sum(
        jnp.where(jnp.arange(leaves)[None, :] == request_ids[:, None], mid_of[None, :], 0), axis=1
    )
    root_ids = jnp.sum(
        jnp.where(jnp.arange(middles_all)[None, :] == middles[:, None], root_of[None, :], 0), axis=1
    )
    path_nodes = jnp.stack(
        [root_ids, roots_all + middles, roots_all + middles_all + request_ids], axis=1
    )
    picked = jnp.arange(nodes_all)[None, None, :] == path_nodes[:, :, None]
    lower_end = jnp.sum(jnp.where(picked, firsts[None, None, :], 0), axis=2)
    upper_end = lower_end + jnp.sum(jnp.where(picked, node_blocks[None, None, :], 0), axis=2)
    return (lower_end, upper_end)


def stage_kernel(n_pieces, own, first, last, base, *refs):
    refs = list(refs)
    lo_ref, hi_ref, ids_ref, q_ref = refs[:4]
    refs = refs[4:]
    if first:
        sfx_ref = refs.pop(0)
    else:
        m_in, l_in, acc_in = refs[:3]
        refs = refs[3:]
    pieces = refs[:n_pieces]
    refs = refs[n_pieces:]
    if last:
        out_ref = refs.pop(0)
        m_ref, l_ref, acc_ref = m_in, l_in, acc_in
    else:
        m_ref, l_ref, acc_ref = refs[:3]
        refs = refs[3:]
    kv_ref, list_ref, sems = refs
    nreq, heads = q_ref.shape[0], q_ref.shape[1]
    coef = LOG2E * q_ref.shape[-1] ** (-0.5)

    copies = []
    for i, piece in enumerate(pieces):
        copy = pltpu.make_async_copy(piece, kv_ref.at[pl.ds(i * own, own)], sems.at[i])
        copy.start()
        copies.append(copy)

    def scores(keys, rows):
        return lax.dot_general(
            keys, rows, (((1,), (1,)), ((), ())), preferred_element_type=jnp.float32
        )

    if first:
        size = sfx_ref.shape[2]
        key_at = lax.broadcasted_iota(jnp.int32, (size, size), 0)
        row_at = lax.broadcasted_iota(jnp.int32, (size, size), 1)

        def start(j, carry):
            keys, values = sfx_ref[j, 0], sfx_ref[j, 1].T
            for h in range(heads):
                s = jnp.where(key_at <= row_at, scores(keys, q_ref[j, h]), NEG)
                top = jnp.max(s, axis=0, keepdims=True)
                p = jnp.exp2((s - top) * coef)
                m_ref[j, pl.ds(h, 1), :] = top
                l_ref[j, pl.ds(h, 1), :] = jnp.sum(p, axis=0, keepdims=True)
                acc_ref[j, h] = jnp.dot(
                    values, p.astype(jnp.bfloat16), preferred_element_type=jnp.float32
                )
            return carry

        lax.fori_loop(0, nreq, start, 0)
    else:
        if not last:
            m_ref[...] = m_in[...]
            l_ref[...] = l_in[...]

    for copy in copies:
        copy.wait()

    def absorb(j, at, count):
        slots = [list_ref[at + u] for u in range(count)]
        keys = jnp.concatenate([kv_ref[s, 0] for s in slots], axis=0)
        values = jnp.concatenate([kv_ref[s, 1] for s in slots], axis=1)
        for h in range(heads):
            s = scores(keys, q_ref[j, h])
            before = m_ref[j, pl.ds(h, 1), :]
            top = jnp.maximum(before, jnp.max(s, axis=0, keepdims=True))
            p = jnp.exp2((s - top) * coef)
            factor = jnp.exp2((before - top) * coef)
            m_ref[j, pl.ds(h, 1), :] = top
            l_ref[j, pl.ds(h, 1), :] = l_ref[j, pl.ds(h, 1), :] * factor + jnp.sum(
                p, axis=0, keepdims=True
            )
            acc_ref[j, h] = acc_ref[j, h] * factor + jnp.dot(
                values, p.astype(jnp.bfloat16), preferred_element_type=jnp.float32
            )

    def request(j, carry):
        r = base + j
        ends = [(lo_ref[r, n], hi_ref[r, n]) for n in range(3)]

        def collect(slot, count):
            block = ids_ref[slot // own] * own + slot % own
            seen = (block >= ends[0][0]) & (block < ends[0][1])
            for low, high in ends[1:]:
                seen = seen | ((block >= low) & (block < high))
            list_ref[count] = slot
            return count + seen.astype(jnp.int32)

        count = lax.fori_loop(0, n_pieces * own, collect, jnp.int32(0))
        quads = count // 4

        def four(i, c):
            absorb(j, 4 * i, 4)
            return c

        lax.fori_loop(0, quads, four, 0)
        rest = count - 4 * quads

        @pl.when(rest >= 2)
        def _():
            absorb(j, 4 * quads, 2)

        @pl.when(rest % 2 == 1)
        def _():
            absorb(j, count - 1, 1)

        if last:
            for h in range(heads):
                done = acc_ref[j, h] * (1.0 / l_ref[j, pl.ds(h, 1), :])
                out_ref[j, :, h * done.shape[0] : (h + 1) * done.shape[0]] = done.T.astype(
                    jnp.bfloat16
                )
        return carry

    if not first and not last:
        acc_ref[...] = acc_in[...]
    lax.fori_loop(0, nreq, request, 0)


SMEM = pl.BlockSpec(memory_space=pltpu.SMEM)
VMEM = pl.BlockSpec(memory_space=pltpu.VMEM)
ANY = pl.BlockSpec(memory_space=pl.ANY)


def stage(lo, hi, ids, q, state, pieces, suffix=None, part=None):
    own, block_tokens, head_dim = pieces[0].shape[0], pieces[0].shape[2], pieces[0].shape[3]
    nreq, heads, rows, _ = q.shape
    first, last = suffix is not None, part is not None
    scratch = [
        pltpu.VMEM((len(pieces) * own, 2, block_tokens, head_dim), jnp.bfloat16),
        pltpu.SMEM((len(pieces) * own + 1,), jnp.int32),
        pltpu.SemaphoreType.DMA((len(pieces),)),
    ]
    params = pltpu.CompilerParams(vmem_limit_bytes=48 * 1024 * 1024)
    stats = jax.ShapeDtypeStruct((nreq, heads, rows), jnp.float32)
    total = jax.ShapeDtypeStruct((nreq, heads, head_dim, rows), jnp.float32)
    if not last:
        body = functools.partial(stage_kernel, len(pieces), own, first, False, 0)
        extra = [suffix] if first else list(state)
        return pl.pallas_call(
            body,
            in_specs=[SMEM] * 3 + [VMEM] * (1 + len(extra)) + [ANY] * len(pieces),
            out_specs=[VMEM] * 3,
            out_shape=[stats, stats, total],
            scratch_shapes=scratch,
            compiler_params=params,
        )(lo, hi, ids, q, *extra, *pieces)
    half = nreq // 2
    body = functools.partial(stage_kernel, len(pieces), own, False, True, part * half)
    return pl.pallas_call(
        body,
        grid=(1,),
        in_specs=[SMEM] * 3
        + [
            pl.BlockSpec((half, heads, rows, head_dim), lambda i: (part, 0, 0, 0)),
            pl.BlockSpec((half, heads, rows), lambda i: (part, 0, 0)),
            pl.BlockSpec((half, heads, rows), lambda i: (part, 0, 0)),
            pl.BlockSpec((half, heads, head_dim, rows), lambda i: (part, 0, 0, 0)),
        ]
        + [ANY] * len(pieces),
        out_specs=pl.BlockSpec((half, rows, heads * head_dim), lambda i: (0, 0, 0)),
        out_shape=jax.ShapeDtypeStruct((half, rows, heads * head_dim), jnp.bfloat16),
        scratch_shapes=scratch,
        compiler_params=params,
    )(lo, hi, ids, q, *state, *pieces)


def on_device(ring, mems, queries, suffix_kv, prefix_kv, out_weight, node_blocks, root_of, mid_of):
    group = lax.axis_index("grp")
    mem = lax.axis_index("mem")
    chips = len(ring)
    core = group % CORES
    chip = group // CORES
    tokens_dev, heads_dev, head_dim = queries.shape
    reqs = tokens_dev // SUFFIX
    heads = heads_dev // CORES
    per_kv = QH // KVH
    own = prefix_kv.shape[0]

    swap = [(2 * s + c, 2 * s + 1 - c) for s in range(chips) for c in range(CORES)]
    ahead = [
        (2 * ring[i] + c, 2 * ring[(i + 1) % chips] + c) for i in range(chips) for c in range(CORES)
    ]
    behind = [(b, a) for a, b in ahead]

    def kv_head(c):
        return (mem * heads_dev + c * heads) // per_kv

    def block_part(c):
        part = lax.dynamic_index_in_dim(prefix_kv, kv_head(c), 3, keepdims=False)
        return jnp.stack([part[:, 0], jnp.swapaxes(part[:, 1], 1, 2)], axis=1)

    own_a = block_part(core)
    own_b = lax.ppermute(block_part(1 - core), "grp", swap)

    order = (jnp.arange(reqs) + mem + 1) % reqs if mems == 2 else jnp.arange(reqs)

    def ordered(x):
        x = x.reshape((reqs, SUFFIX) + x.shape[1:])
        return jnp.stack(
            [lax.dynamic_index_in_dim(x, order[k], 0, keepdims=False) for k in range(reqs)]
        )

    q_ordered = jnp.transpose(ordered(queries), (0, 2, 1, 3))

    def query_part(c):
        return lax.dynamic_slice_in_dim(q_ordered, c * heads, heads, 1)

    def suffix_part(c):
        part = lax.dynamic_index_in_dim(suffix_kv, kv_head(c), 2, keepdims=False)
        return jnp.transpose(ordered(part), (0, 2, 1, 3))

    def interleave(mine, theirs):
        return jnp.stack([mine, theirs], axis=1).reshape((2 * reqs,) + mine.shape[1:])

    q = interleave(query_part(core), lax.ppermute(query_part(1 - core), "grp", swap))
    suffix = interleave(suffix_part(core), lax.ppermute(suffix_part(1 - core), "grp", swap))

    both = jnp.stack([group, group ^ 1])
    request_ids = (both[None, :] * reqs + order[:, None]).reshape(-1)
    lo, hi = path_ranges(request_ids, node_blocks, root_of, mid_of)

    place = jnp.sum(jnp.where(jnp.asarray(ring) == chip, jnp.arange(chips), 0))

    def source(step):
        at = (place + step) % chips
        return jnp.sum(jnp.where(jnp.arange(chips) == at, jnp.asarray(ring), 0))

    def ids(*steps):
        return jnp.stack([CORES * source(s) + (core ^ side) for s, side in steps]).astype(jnp.int32)

    forth, back = [own_a, own_b], [own_a, own_b]
    received = []
    for k in range(1, (chips - 2) // 2 + 1):
        forth = [lax.ppermute(x, "grp", ahead) for x in forth]
        back = [lax.ppermute(x, "grp", behind) for x in back]
        received.append((ids((-k, 0), (-k, 1), (k, 0), (k, 1)), forth + back))
    k = chips // 2
    final = [lax.ppermute(forth[0], "grp", ahead), lax.ppermute(back[1], "grp", behind)]
    final_ids = ids((-k, 0), (k, 1))

    state = stage(lo, hi, ids((0, 0), (0, 1)), q, None, [own_a, own_b], suffix=suffix)
    for piece_ids, pieces in received:
        state = stage(lo, hi, piece_ids, q, state, pieces)

    def attended(part):
        done = stage(lo, hi, final_ids, q, state, final, part=part)
        theirs = lax.ppermute(done[1], "grp", swap)
        mine = done[0]
        return jnp.where(
            core == 0,
            jnp.concatenate([mine, theirs], axis=1),
            jnp.concatenate([theirs, mine], axis=1),
        )

    return attended, out_weight


def finish(attended, out_weight, mems):
    def project(rows):
        return jnp.dot(rows, out_weight, preferred_element_type=jnp.float32)

    if mems != 2:
        rows = jnp.concatenate([attended(0), attended(1)], axis=0)
        return lax.psum_scatter(
            project(rows).astype(jnp.bfloat16), "mem", scatter_dimension=0, tiled=True
        )
    sent = project(attended(0)).astype(jnp.bfloat16)
    got = lax.ppermute(sent, "mem", [(0, 1), (1, 0)])
    kept = project(attended(1))
    return (kept + got.astype(jnp.float32)).astype(jnp.bfloat16)


def solution(mesh):
    chips = mesh.shape["grp"] // CORES
    mems = mesh.shape["mem"]
    if chips == 8:
        ring = [0, 2, 4, 6, 7, 5, 3, 1]
    else:
        ring = list(range(chips // 2)) + list(range(chips // 2, chips))[::-1]

    def body(*args):
        attended, out_weight = on_device(ring, mems, *args)
        return finish(attended, out_weight, mems)

    return jax.shard_map(
        body,
        mesh=mesh,
        in_specs=(
            P("grp", "mem", None),
            P("grp", None, None, None),
            P("grp", None, None, None, None),
            P("mem", None),
            P(),
            P(),
            P(),
        ),
        out_specs=P(("grp", "mem"), None),
        check_vma=False,
    )
```

```python
import functools

import jax
import jax.numpy as jnp
from jax import lax
from jax.experimental import pallas as pl
from jax.experimental.pallas import tpu as pltpu
from jax.sharding import PartitionSpec as P

QH = 32
KVH = 4
SUFFIX = 256
CORES = 2
NEG = -1e30


def path_ranges(request_ids, node_blocks, root_of, mid_of):
    nodes_all = node_blocks.shape[0]
    middles_all = root_of.shape[0]
    leaves = mid_of.shape[0]
    roots_all = nodes_all - middles_all - leaves
    firsts = jnp.cumsum(node_blocks) - node_blocks
    middles = jnp.sum(
        jnp.where(jnp.arange(leaves)[None, :] == request_ids[:, None], mid_of[None, :], 0), axis=1
    )
    root_ids = jnp.sum(
        jnp.where(jnp.arange(middles_all)[None, :] == middles[:, None], root_of[None, :], 0), axis=1
    )
    path_nodes = jnp.stack(
        [root_ids, roots_all + middles, roots_all + middles_all + request_ids], axis=1
    )
    picked = jnp.arange(nodes_all)[None, None, :] == path_nodes[:, :, None]
    lower_end = jnp.sum(jnp.where(picked, firsts[None, None, :], 0), axis=2)
    upper_end = lower_end + jnp.sum(jnp.where(picked, node_blocks[None, None, :], 0), axis=2)
    return (lower_end, upper_end)


def stage_kernel(n_pieces, own, first, last, base, *refs):
    refs = list(refs)
    count_ref, list_ref, mine_ref, theirs_ref = refs[:4]
    refs = refs[4:]
    if first:
        suffix_refs, refs = refs[:2], refs[2:]
    else:
        m_in, l_in, acc_in = refs[:3]
        refs = refs[3:]
    pieces, refs = refs[:n_pieces], refs[n_pieces:]
    if last:
        out_ref = refs.pop(0)
        m_ref, l_ref = m_in, l_in
    else:
        m_ref, l_ref, acc_out = refs[:3]
        refs = refs[3:]
    kv_ref, q_ref, acc_ref, piece_sems, q_sems, in_sems, out_sems = refs
    nreq, heads, rows, head_dim = q_ref.shape
    scale = head_dim ** (-0.5)

    def q_copy(j):
        source = (mine_ref, theirs_ref)[j % 2].at[(base + j) // 2]
        return pltpu.make_async_copy(source, q_ref.at[j], q_sems.at[j])

    def acc_copy(j):
        return pltpu.make_async_copy(acc_in.at[base + j], acc_ref.at[j], in_sems.at[j])

    def out_copy(j):
        return pltpu.make_async_copy(acc_ref.at[j], acc_out.at[j], out_sems.at[j])

    def piece_copy(i):
        return pltpu.make_async_copy(
            pieces[i], kv_ref.at[pl.ds(i * own, own)], piece_sems.at[i]
        )

    def active(j):
        return count_ref[base + j] > 0

    if first:
        for j in range(nreq):
            q_copy(j).start()
    for i in range(n_pieces):
        piece_copy(i).start()
    if not first:
        m_values, l_values = m_in[...], l_in[...]
        for j in range(nreq):

            @pl.when(active(j))
            def _():
                q_copy(j).start()
                acc_copy(j).start()

            if last:

                @pl.when(jnp.logical_not(active(j)))
                def _():
                    acc_copy(j).start()

        if not last:
            m_ref[...] = m_values
            l_ref[...] = l_values

    def dot(a, b):
        return jnp.dot(a, b, preferred_element_type=jnp.float32)

    def sweep(j, keys, values, old, mask=None):
        scores, weights, tops, totals = {}, {}, [], []
        if old is not None:
            highest, sums = m_ref[j], l_ref[j]
        for t in range(heads + 3):
            if t < heads:
                scores[t] = lax.dot_general(
                    keys, q_ref[j, t], (((1,), (1,)), ((), ())), preferred_element_type=jnp.float32
                )
            h = t - 3
            if h >= 0:
                p, factor = weights.pop(h)
                if factor is None:
                    acc_ref[j, h] = dot(values, p)
                else:
                    acc_ref[j, h] = acc_ref[j, h] * factor + dot(values, p)
            h = t - 2
            if 0 <= h < heads:
                s = scores.pop(h)
                if mask is not None:
                    s = jnp.where(mask, s, NEG)
                top = jnp.max(s, axis=0, keepdims=True)
                if old is None:
                    factor = None
                    p = jnp.exp((s - top) * scale)
                    total = jnp.sum(p, axis=0, keepdims=True)
                else:
                    before = highest[h : h + 1]
                    top = jnp.maximum(before, top)
                    p = jnp.exp((s - top) * scale)
                    factor = jnp.exp((before - top) * scale)
                    total = sums[h : h + 1] * factor + jnp.sum(p, axis=0, keepdims=True)
                tops.append(top)
                totals.append(total)
                weights[h] = (p.astype(jnp.bfloat16), factor)
        m_ref[j] = jnp.concatenate(tops, axis=0)
        l_ref[j] = jnp.concatenate(totals, axis=0)

    if first:
        key_at = lax.broadcasted_iota(jnp.int32, (rows, rows), 0)
        row_at = lax.broadcasted_iota(jnp.int32, (rows, rows), 1)
        for j in range(nreq):
            q_copy(j).wait()
        for side in range(2):

            def start(k, carry, side=side):
                sfx = suffix_refs[side]
                sweep(2 * k + side, sfx[k, 0], sfx[k, 1].T, None, key_at <= row_at)
                return carry

            lax.fori_loop(0, nreq // 2, start, 0)

    for i in range(n_pieces):
        piece_copy(i).wait()

    def absorb(j, at, count):
        slots = [list_ref[base + j, at + u] for u in range(count)]
        keys = jnp.concatenate([kv_ref[s, 0] for s in slots], axis=0)
        values = jnp.concatenate([kv_ref[s, 1] for s in slots], axis=0).T
        sweep(j, keys, values, True)

    for j in range(nreq):
        if not first:

            @pl.when(active(j))
            def _():
                q_copy(j).wait()
                acc_copy(j).wait()

            if last:

                @pl.when(jnp.logical_not(active(j)))
                def _():
                    acc_copy(j).wait()

    def request(j, carry):
        count = count_ref[base + j]
        groups = count // 8

        def eight(i, c):
            absorb(j, 8 * i, 8)
            return c

        lax.fori_loop(0, groups, eight, 0)
        for size in (4, 2, 1):

            @pl.when((count // size) % 2 == 1)
            def _():
                absorb(j, (count // (2 * size)) * (2 * size), size)

        return carry

    lax.fori_loop(0, nreq, request, 0)

    if last:
        for j in range(nreq):
            for h in range(heads):
                done = acc_ref[j, h] * (1.0 / l_ref[j, pl.ds(h, 1), :])
                out_ref[j, h * head_dim : (h + 1) * head_dim, :] = done.astype(jnp.bfloat16)
        return
    for j in range(nreq):
        if first:
            out_copy(j).start()
        else:

            @pl.when(active(j))
            def _():
                out_copy(j).start()

    for j in range(nreq):
        if first:
            out_copy(j).wait()
        else:

            @pl.when(active(j))
            def _():
                out_copy(j).wait()


SMEM = pl.BlockSpec(memory_space=pltpu.SMEM)
VMEM = pl.BlockSpec(memory_space=pltpu.VMEM)
ANY = pl.BlockSpec(memory_space=pl.ANY)


def stage(work, queries, state, pieces, suffix=None, part=None):
    counts, lists = work
    own, _, block_tokens, head_dim = pieces[0].shape
    half, heads, rows, _ = queries[0].shape
    first, last = suffix is not None, part is not None
    nreq = half if last else 2 * half
    base = part * half if last else 0
    scratch = [
        pltpu.VMEM((len(pieces) * own, 2, block_tokens, head_dim), jnp.bfloat16),
        pltpu.VMEM((nreq, heads, rows, head_dim), jnp.bfloat16),
        pltpu.VMEM((nreq, heads, head_dim, rows), jnp.float32),
        pltpu.SemaphoreType.DMA((len(pieces),)),
        pltpu.SemaphoreType.DMA((nreq,)),
        pltpu.SemaphoreType.DMA((nreq,)),
        pltpu.SemaphoreType.DMA((nreq,)),
    ]
    params = pltpu.CompilerParams(vmem_limit_bytes=48 * 1024 * 1024)
    body = functools.partial(stage_kernel, len(pieces), own, first, last, base)
    head_specs = [SMEM, SMEM, ANY, ANY]
    if last:
        stat = pl.BlockSpec((nreq, heads, rows), lambda i: (part, 0, 0))
        return pl.pallas_call(
            body,
            grid=(1,),
            in_specs=head_specs + [stat, stat, ANY] + [ANY] * len(pieces),
            out_specs=pl.BlockSpec((nreq, heads * head_dim, rows), lambda i: (0, 0, 0)),
            out_shape=jax.ShapeDtypeStruct((nreq, heads * head_dim, rows), jnp.bfloat16),
            scratch_shapes=scratch,
            compiler_params=params,
        )(counts, lists, *queries, *state, *pieces)
    stats = jax.ShapeDtypeStruct((nreq, heads, rows), jnp.float32)
    total = jax.ShapeDtypeStruct((nreq, heads, head_dim, rows), jnp.float32)
    extra, extra_specs = (suffix, [VMEM] * 2) if first else (state, [VMEM, VMEM, ANY])
    return pl.pallas_call(
        body,
        in_specs=head_specs + extra_specs + [ANY] * len(pieces),
        out_specs=[VMEM, VMEM, ANY],
        out_shape=[stats, stats, total],
        scratch_shapes=scratch,
        compiler_params=params,
        input_output_aliases={} if first else {6: 2},
    )(counts, lists, *queries, *extra, *pieces)


def on_device(ring, mems, queries, suffix_kv, prefix_kv, out_weight, node_blocks, root_of, mid_of):
    group = lax.axis_index("grp")
    mem = lax.axis_index("mem")
    chips = len(ring)
    core = group % CORES
    chip = group // CORES
    tokens_dev, heads_dev, head_dim = queries.shape
    reqs = tokens_dev // SUFFIX
    heads = heads_dev // CORES
    per_kv = QH // KVH
    own = prefix_kv.shape[0]

    swap = [(2 * s + c, 2 * s + 1 - c) for s in range(chips) for c in range(CORES)]
    ahead = [
        (2 * ring[i] + c, 2 * ring[(i + 1) % chips] + c) for i in range(chips) for c in range(CORES)
    ]
    behind = [(b, a) for a, b in ahead]

    def kv_head(c):
        return (mem * heads_dev + c * heads) // per_kv

    def block_part(c):
        return lax.dynamic_index_in_dim(prefix_kv, kv_head(c), 3, keepdims=False)

    own_a = block_part(core)
    own_b = lax.ppermute(block_part(1 - core), "grp", swap)

    own_b, queries, suffix_kv, node_blocks = lax.optimization_barrier(
        (own_b, queries, suffix_kv, node_blocks)
    )

    order = (jnp.arange(reqs) + mem + 1) % reqs if mems == 2 else jnp.arange(reqs)

    def ordered(x):
        x = x.reshape((reqs, SUFFIX) + x.shape[1:])
        return jnp.stack(
            [lax.dynamic_index_in_dim(x, order[k], 0, keepdims=False) for k in range(reqs)]
        )

    def query_part(c):
        return lax.dynamic_slice_in_dim(q_ordered, c * heads, heads, 1)

    def suffix_part(c):
        part = lax.dynamic_index_in_dim(suffix_kv, kv_head(c), 2, keepdims=False)
        return jnp.transpose(ordered(part), (0, 2, 1, 3))

    q_ordered = jnp.transpose(ordered(queries), (0, 2, 1, 3))
    q = [query_part(core), lax.ppermute(query_part(1 - core), "grp", swap)]
    suffix = [suffix_part(core), lax.ppermute(suffix_part(1 - core), "grp", swap)]

    both = jnp.stack([group, group ^ 1])
    request_ids = (both[None, :] * reqs + order[:, None]).reshape(-1)
    lo, hi = path_ranges(request_ids, node_blocks, root_of, mid_of)

    place = jnp.sum(jnp.where(jnp.asarray(ring) == chip, jnp.arange(chips), 0))

    def work(*steps):
        ids = []
        for step, side in steps:
            at = (place + step) % chips
            source = jnp.sum(jnp.where(jnp.arange(chips) == at, jnp.asarray(ring), 0))
            ids.append(CORES * source + (core ^ side))
        blocks = (jnp.stack(ids)[:, None] * own + jnp.arange(own)[None, :]).reshape(-1)
        inside = (blocks[None, None, :] >= lo[:, :, None]) & (blocks[None, None, :] < hi[:, :, None])
        seen = jnp.any(inside, axis=1)
        slots = jnp.arange(blocks.shape[0])
        rank = jnp.sum(seen[:, None, :] & (slots[None, None, :] < slots[None, :, None]), axis=2)
        here = seen[:, :, None] & (rank[:, :, None] == slots[None, None, :])
        lists = jnp.sum(jnp.where(here, slots[None, :, None], 0), axis=1)
        return jnp.sum(seen, axis=1).astype(jnp.int32), lists.astype(jnp.int32)

    state = stage(work((0, 0), (0, 1)), q, None, [own_a, own_b], suffix=suffix)
    forth, back = [own_a, own_b], [own_a, own_b]
    for k in range(1, (chips - 2) // 2 + 1):
        forth = [lax.ppermute(x, "grp", ahead) for x in forth]
        back = [lax.ppermute(x, "grp", behind) for x in back]
        forth[1], back[1], state = lax.optimization_barrier((forth[1], back[1], state))
        state = stage(work((-k, 0), (-k, 1), (k, 0), (k, 1)), q, state, forth + back)
    k = chips // 2
    final = [lax.ppermute(forth[0], "grp", ahead), lax.ppermute(back[1], "grp", behind)]
    final_work = work((-k, 0), (k, 1))

    def attended(part):
        done = stage(final_work, q, state, final, part=part)
        theirs = lax.ppermute(done[1], "grp", swap)
        mine = done[0]
        return jnp.where(
            core == 0,
            jnp.concatenate([mine, theirs], axis=0),
            jnp.concatenate([theirs, mine], axis=0),
        )

    return attended, out_weight


def finish(attended, out_weight, mems):
    def project(rows):
        return lax.dot_general(
            rows, out_weight, (((0,), (0,)), ((), ())), preferred_element_type=jnp.float32
        )

    if mems != 2:
        rows = jnp.concatenate([attended(0), attended(1)], axis=1)
        return lax.psum_scatter(
            project(rows).astype(jnp.bfloat16), "mem", scatter_dimension=0, tiled=True
        )
    sent = project(attended(0)).astype(jnp.bfloat16)
    got = lax.ppermute(sent, "mem", [(0, 1), (1, 0)])
    kept = project(attended(1))
    return (kept + got.astype(jnp.float32)).astype(jnp.bfloat16)


def solution(mesh):
    chips = mesh.shape["grp"] // CORES
    mems = mesh.shape["mem"]
    if chips == 8:
        ring = [0, 2, 4, 6, 7, 5, 3, 1]
    else:
        ring = list(range(chips // 2)) + list(range(chips // 2, chips))[::-1]

    def body(*args):
        attended, out_weight = on_device(ring, mems, *args)
        return finish(attended, out_weight, mems)

    return jax.shard_map(
        body,
        mesh=mesh,
        in_specs=(
            P("grp", "mem", None),
            P("grp", None, None, None),
            P("grp", None, None, None, None),
            P("mem", None),
            P(),
            P(),
            P(),
        ),
        out_specs=P(("grp", "mem"), None),
        check_vma=False,
    )
```

```python
import functools

import jax
import jax.numpy as jnp
from jax import lax
from jax.experimental import pallas as pl
from jax.experimental.pallas import tpu as pltpu
from jax.sharding import PartitionSpec as P

QH = 32
KVH = 4
SUFFIX = 256
CORES = 2
NEG = -1e30


def path_ranges(request_ids, node_blocks, root_of, mid_of):
    nodes_all = node_blocks.shape[0]
    middles_all = root_of.shape[0]
    leaves = mid_of.shape[0]
    roots_all = nodes_all - middles_all - leaves
    firsts = jnp.cumsum(node_blocks) - node_blocks
    middles = jnp.sum(
        jnp.where(jnp.arange(leaves)[None, :] == request_ids[:, None], mid_of[None, :], 0), axis=1
    )
    root_ids = jnp.sum(
        jnp.where(jnp.arange(middles_all)[None, :] == middles[:, None], root_of[None, :], 0), axis=1
    )
    path_nodes = jnp.stack(
        [root_ids, roots_all + middles, roots_all + middles_all + request_ids], axis=1
    )
    picked = jnp.arange(nodes_all)[None, None, :] == path_nodes[:, :, None]
    lower_end = jnp.sum(jnp.where(picked, firsts[None, None, :], 0), axis=2)
    upper_end = lower_end + jnp.sum(jnp.where(picked, node_blocks[None, None, :], 0), axis=2)
    return (lower_end, upper_end)


def stage_kernel(n_pieces, own, number, first, last, base, *refs):
    refs = list(refs)
    count_ref, list_ref, mine_ref, theirs_ref = refs[:4]
    refs = refs[4:]
    if first:
        suffix_refs, refs = refs[:2], refs[2:]
    else:
        m_in, l_in, acc_in = refs[:3]
        refs = refs[3:]
    pieces, refs = refs[:n_pieces], refs[n_pieces:]
    if last:
        out_ref = refs.pop(0)
        m_ref, l_ref = m_in, l_in
    else:
        m_ref, l_ref, acc_out = refs[:3]
        refs = refs[3:]
    kv_ref, q_ref, acc_ref, piece_sems, q_sems, in_sems, out_sems = refs
    nreq, heads, rows, head_dim = q_ref.shape
    scale = head_dim ** (-0.5)

    def q_copy(j):
        source = (mine_ref, theirs_ref)[(base + j) % 2].at[(base + j) // 2]
        return pltpu.make_async_copy(source, q_ref.at[j], q_sems.at[j])

    def acc_copy(j):
        return pltpu.make_async_copy(acc_in.at[base + j], acc_ref.at[j], in_sems.at[j])

    def out_copy(j):
        return pltpu.make_async_copy(acc_ref.at[j], acc_out.at[j], out_sems.at[j])

    def piece_copy(i):
        return pltpu.make_async_copy(
            pieces[i], kv_ref.at[pl.ds(i * own, own)], piece_sems.at[i]
        )

    def active(j):
        return count_ref[number, base + j] > 0

    if first:
        for j in range(nreq):
            q_copy(j).start()
    for i in range(n_pieces):
        piece_copy(i).start()
    if not first:
        m_values, l_values = m_in[...], l_in[...]
        for j in range(nreq):

            @pl.when(active(j))
            def _():
                q_copy(j).start()
                acc_copy(j).start()

            if last:

                @pl.when(jnp.logical_not(active(j)))
                def _():
                    acc_copy(j).start()

        if not last:
            m_ref[...] = m_values
            l_ref[...] = l_values

    def dot(a, b):
        return jnp.dot(a, b, preferred_element_type=jnp.float32)

    def sweep(j, keys, values, old, mask=None):
        size = values.shape[0]
        values = jnp.concatenate([values.T, jnp.ones((16, size), jnp.bfloat16)], axis=0)
        scores, weights, tops, totals = {}, {}, [], []
        if old:
            highest, sums = m_ref[j], l_ref[j]
        for t in range(heads + 3):
            if t < heads:
                scores[t] = lax.dot_general(
                    keys, q_ref[j, t], (((1,), (1,)), ((), ())), preferred_element_type=jnp.float32
                )
            h = t - 3
            if h >= 0:
                p, factor = weights.pop(h)
                summed = dot(values, p)
                total = summed[head_dim : head_dim + 1]
                if old:
                    acc_ref[j, h] = acc_ref[j, h] * factor + summed[:head_dim]
                    total = sums[h : h + 1] * factor + total
                else:
                    acc_ref[j, h] = summed[:head_dim]
                totals.append(total)
            h = t - 2
            if 0 <= h < heads:
                s = scores.pop(h)
                if mask is not None:
                    s = jnp.where(mask, s, NEG)
                top = jnp.max(s, axis=0, keepdims=True)
                factor = None
                if old:
                    before = highest[h : h + 1]
                    top = jnp.maximum(before, top)
                    factor = jnp.exp((before - top) * scale)
                tops.append(top)
                p = jnp.exp((s - top).astype(jnp.bfloat16) * jnp.bfloat16(scale))
                weights[h] = (p, factor)
        m_ref[j] = jnp.concatenate(tops, axis=0)
        l_ref[j] = jnp.concatenate(totals, axis=0)

    if first:
        key_at = lax.broadcasted_iota(jnp.int32, (rows, rows), 0)
        row_at = lax.broadcasted_iota(jnp.int32, (rows, rows), 1)
        for j in range(nreq):
            q_copy(j).wait()
        for side in range(2):

            def start(k, carry, side=side):
                sfx = suffix_refs[side]
                sweep(2 * k + side, sfx[k, 0], sfx[k, 1], False, key_at <= row_at)
                return carry

            lax.fori_loop(0, nreq // 2, start, 0)

    for i in range(n_pieces):
        piece_copy(i).wait()

    def absorb(j, at, count):
        slots = [list_ref[number, base + j, at + u] for u in range(count)]
        keys = jnp.concatenate([kv_ref[s, 0] for s in slots], axis=0)
        values = jnp.concatenate([kv_ref[s, 1] for s in slots], axis=0)
        sweep(j, keys, values, True)

    for j in range(nreq):
        if not first:

            @pl.when(active(j))
            def _():
                q_copy(j).wait()
                acc_copy(j).wait()

            if last:

                @pl.when(jnp.logical_not(active(j)))
                def _():
                    acc_copy(j).wait()

    def request(j, carry):
        count = count_ref[number, base + j]
        groups = count // 8

        def eight(i, c):
            absorb(j, 8 * i, 8)
            return c

        lax.fori_loop(0, groups, eight, 0)
        for size in (4, 2, 1):

            @pl.when((count // size) % 2 == 1)
            def _():
                absorb(j, (count // (2 * size)) * (2 * size), size)

        return carry

    lax.fori_loop(0, nreq, request, 0)

    if last:
        for j in range(nreq):
            for h in range(heads):
                done = acc_ref[j, h] * (1.0 / l_ref[j, pl.ds(h, 1), :])
                out_ref[:, h * head_dim : (h + 1) * head_dim] = done.astype(jnp.bfloat16).T
        return
    for j in range(nreq):
        if first:
            out_copy(j).start()
        else:

            @pl.when(active(j))
            def _():
                out_copy(j).start()

    for j in range(nreq):
        if first:
            out_copy(j).wait()
        else:

            @pl.when(active(j))
            def _():
                out_copy(j).wait()


SMEM = pl.BlockSpec(memory_space=pltpu.SMEM)
VMEM = pl.BlockSpec(memory_space=pltpu.VMEM)
ANY = pl.BlockSpec(memory_space=pl.ANY)


def stage(number, work, queries, state, pieces, suffix=None, request=None):
    counts, lists = work
    own, _, block_tokens, head_dim = pieces[0].shape
    half, heads, rows, _ = queries[0].shape
    first, last = suffix is not None, request is not None
    nreq = 1 if last else 2 * half
    base = request if last else 0
    scratch = [
        pltpu.VMEM((len(pieces) * own, 2, block_tokens, head_dim), jnp.bfloat16),
        pltpu.VMEM((nreq, heads, rows, head_dim), jnp.bfloat16),
        pltpu.VMEM((nreq, heads, head_dim, rows), jnp.float32),
        pltpu.SemaphoreType.DMA((len(pieces),)),
        pltpu.SemaphoreType.DMA((nreq,)),
        pltpu.SemaphoreType.DMA((nreq,)),
        pltpu.SemaphoreType.DMA((nreq,)),
    ]
    params = pltpu.CompilerParams(vmem_limit_bytes=48 * 1024 * 1024)
    body = functools.partial(stage_kernel, len(pieces), own, number, first, last, base)
    head_specs = [SMEM, SMEM, ANY, ANY]
    if last:
        stat = pl.BlockSpec((nreq, heads, rows), lambda i: (request, 0, 0))
        return pl.pallas_call(
            body,
            grid=(1,),
            in_specs=head_specs + [stat, stat, ANY] + [ANY] * len(pieces),
            out_specs=pl.BlockSpec((rows, heads * head_dim), lambda i: (0, 0)),
            out_shape=jax.ShapeDtypeStruct((rows, heads * head_dim), jnp.bfloat16),
            scratch_shapes=scratch,
            compiler_params=params,
        )(counts, lists, *queries, *state, *pieces)
    stats = jax.ShapeDtypeStruct((nreq, heads, rows), jnp.float32)
    total = jax.ShapeDtypeStruct((nreq, heads, head_dim, rows), jnp.float32)
    extra, extra_specs = (suffix, [VMEM] * 2) if first else (state, [VMEM, VMEM, ANY])
    return pl.pallas_call(
        body,
        in_specs=head_specs + extra_specs + [ANY] * len(pieces),
        out_specs=[VMEM, VMEM, ANY],
        out_shape=[stats, stats, total],
        scratch_shapes=scratch,
        compiler_params=params,
        input_output_aliases={} if first else {6: 2},
    )(counts, lists, *queries, *extra, *pieces)


def project_kernel(core_ref, mine_ref, theirs_ref, weight_ref, out_ref):
    depth = mine_ref.shape[1]
    core = core_ref[0]
    summed = jnp.dot(
        mine_ref[...],
        weight_ref[pl.ds(core * depth, depth), :],
        preferred_element_type=jnp.float32,
    ) + jnp.dot(
        theirs_ref[...],
        weight_ref[pl.ds((1 - core) * depth, depth), :],
        preferred_element_type=jnp.float32,
    )
    out_ref[...] = summed.astype(out_ref.dtype)


def project(core, mine, theirs, out_weight, part, parts, dtype):
    rows, depth = mine.shape
    columns = out_weight.shape[1] // parts
    width = min(512, columns)
    steps = columns // width
    whole = pl.BlockSpec((rows, depth), lambda i, c: (0, 0))
    return pl.pallas_call(
        project_kernel,
        grid_spec=pltpu.PrefetchScalarGridSpec(
            num_scalar_prefetch=1,
            grid=(steps,),
            in_specs=[
                whole,
                whole,
                pl.BlockSpec((out_weight.shape[0], width), lambda i, c: (0, part * steps + i)),
            ],
            out_specs=pl.BlockSpec((rows, width), lambda i, c: (0, i)),
        ),
        out_shape=jax.ShapeDtypeStruct((rows, columns), dtype),
        compiler_params=pltpu.CompilerParams(vmem_limit_bytes=48 * 1024 * 1024),
    )(core.reshape(1), mine, theirs, out_weight)


def ring_order(chips, at):
    half = chips // 2
    if chips == 8:
        place = jnp.where(at % 2 == 0, at // 2, chips - 1 - at // 2)
        chip = jnp.where(at < half, 2 * at, 2 * (chips - 1 - at) + 1)
    else:
        place = jnp.where(at < half, at, chips + half - 1 - at)
        chip = place
    return place, chip


def work_tables(plan, chips, own, group, lo, hi):
    most = max(len(pieces) for pieces in plan)
    filled = [pieces + [(0, -1)] * (most - len(pieces)) for pieces in plan]
    steps = jnp.asarray([[step for step, _ in pieces] for pieces in filled], jnp.int32)
    sides = jnp.asarray([[side for _, side in pieces] for pieces in filled], jnp.int32)
    place = ring_order(chips, group // CORES)[0]
    source = ring_order(chips, (place + steps + chips) % chips)[1]
    device = jnp.where(sides < 0, -chips * CORES, CORES * source + ((group % CORES) ^ sides))
    slots = jnp.arange(most * own)
    blocks = jnp.repeat(device * own, own, axis=1) + (slots % own)[None, :]
    inside = (blocks[:, None, None, :] >= lo[None, :, :, None]) & (
        blocks[:, None, None, :] < hi[None, :, :, None]
    )
    seen = jnp.any(inside, axis=2)
    ahead = slots[None, :] < slots[:, None]
    rank = jnp.sum(jnp.where(seen[:, :, None, :] & ahead, 1, 0), axis=3)
    here = seen[:, :, None, :] & (rank[:, :, None, :] == slots[:, None])
    lists = jnp.sum(jnp.where(here, slots, 0), axis=3)
    return jnp.sum(jnp.where(seen, 1, 0), axis=2).astype(jnp.int32), lists.astype(jnp.int32)


def on_device(chips, mems, queries, suffix_kv, prefix_kv, out_weight, node_blocks, root_of, mid_of):
    group = lax.axis_index("grp")
    mem = lax.axis_index("mem")
    core = group % CORES
    tokens_dev, heads_dev, head_dim = queries.shape
    reqs = tokens_dev // SUFFIX
    heads = heads_dev // CORES
    per_kv = QH // KVH
    own = prefix_kv.shape[0]
    half = chips // 2
    if chips == 8:
        ring = [0, 2, 4, 6, 7, 5, 3, 1]
    else:
        ring = list(range(half)) + list(range(half, chips))[::-1]

    swap = [(2 * s + c, 2 * s + 1 - c) for s in range(chips) for c in range(CORES)]
    ahead = [
        (2 * ring[i] + c, 2 * ring[(i + 1) % chips] + c) for i in range(chips) for c in range(CORES)
    ]
    behind = [(b, a) for a, b in ahead]

    kv_start = mem * heads_dev // per_kv
    kv_count = max(1, heads_dev // per_kv)

    def of_core(heads_kv, c):
        if kv_count == 1:
            return heads_kv[0]
        return jnp.where(c == 0, heads_kv[0], heads_kv[1])

    served = lax.dynamic_slice_in_dim(prefix_kv, kv_start, kv_count, 3)
    served = jnp.transpose(served, (3, 0, 1, 2, 4))
    own_a = of_core(served, core)
    own_b = lax.ppermute(of_core(served, 1 - core), "grp", swap)

    own_b, queries, suffix_kv, node_blocks, group = lax.optimization_barrier(
        (own_b, queries, suffix_kv, node_blocks, group)
    )

    order = (jnp.arange(reqs) + mem + 1) % reqs if mems == 2 else jnp.arange(reqs)

    def ordered(x):
        x = x.reshape((reqs, SUFFIX) + x.shape[1:])
        if mems != 2:
            return x
        return jnp.where(mem == 0, x[::-1], x)

    def query_part(c):
        return lax.dynamic_slice_in_dim(q_ordered, c * heads, heads, 1)

    q_ordered = jnp.transpose(ordered(queries), (0, 2, 1, 3))
    q = [query_part(core), lax.ppermute(query_part(1 - core), "grp", swap)]
    served = lax.dynamic_slice_in_dim(suffix_kv, kv_start, kv_count, 2)
    served = jnp.transpose(ordered(served), (3, 0, 2, 1, 4))
    suffix = [of_core(served, core), lax.ppermute(of_core(served, 1 - core), "grp", swap)]

    both = jnp.stack([group, group ^ 1])
    request_ids = (both[None, :] * reqs + order[:, None]).reshape(-1)
    lo, hi = path_ranges(request_ids, node_blocks, root_of, mid_of)
    far = chips // 2
    plan = [[(0, 0), (0, 1)]]
    plan += [[(-k, 0), (-k, 1), (k, 0), (k, 1)] for k in range(1, far)]
    plan += [[(-far, 0), (far, 1)]]
    work = work_tables(plan, chips, own, group, lo, hi)

    state = stage(0, work, q, None, [own_a, own_b], suffix=suffix)
    forth, back = [own_a, own_b], [own_a, own_b]
    for k in range(1, far):
        forth = [lax.ppermute(x, "grp", ahead) for x in forth]
        back = [lax.ppermute(x, "grp", behind) for x in back]
        forth[1], back[1], state = lax.optimization_barrier((forth[1], back[1], state))
        state = stage(k, work, q, state, forth + back)
    final = [lax.ppermute(forth[0], "grp", ahead), lax.ppermute(back[1], "grp", behind)]

    def attended(part, state):
        leaving = stage(far, work, q, state, final, request=2 * part + 1)
        staying = stage(far, work, q, state, final, request=2 * part)
        return staying, lax.ppermute(leaving, "grp", swap)

    if mems != 2:
        rows = [project(core, *attended(k, state), out_weight, 0, 1, jnp.bfloat16) for k in range(reqs)]
        return lax.psum_scatter(
            jnp.concatenate(rows, axis=0), "mem", scatter_dimension=0, tiled=True
        )
    parts = 2
    leaving = attended(0, state)
    sent = [project(core, *leaving, out_weight, i, parts, jnp.bfloat16) for i in range(parts)]
    sent[-1], state = lax.optimization_barrier((sent[-1], state))
    got = [lax.ppermute(x, "mem", [(0, 1), (1, 0)]) for x in sent]
    kept = project(core, *attended(1, state), out_weight, 0, 1, jnp.float32)
    return (kept + jnp.concatenate(got, axis=1).astype(jnp.float32)).astype(jnp.bfloat16)


def solution(mesh):
    return jax.shard_map(
        functools.partial(on_device, mesh.shape["grp"] // CORES, mesh.shape["mem"]),
        mesh=mesh,
        in_specs=(
            P("grp", "mem", None),
            P("grp", None, None, None),
            P("grp", None, None, None, None),
            P("mem", None),
            P(),
            P(),
            P(),
        ),
        out_specs=P(("grp", "mem"), None),
        check_vma=False,
    )
```

```python
import functools

import jax
import jax.numpy as jnp
from jax import lax
from jax.experimental import pallas as pl
from jax.experimental.pallas import tpu as pltpu
from jax.sharding import PartitionSpec as P

QH = 32
KVH = 4
SUFFIX = 256
CORES = 2
NEG = -1e30


def path_ranges(request_ids, node_blocks, root_of, mid_of):
    nodes_all = node_blocks.shape[0]
    middles_all = root_of.shape[0]
    leaves = mid_of.shape[0]
    roots_all = nodes_all - middles_all - leaves
    firsts = jnp.cumsum(node_blocks) - node_blocks
    middles = jnp.sum(
        jnp.where(jnp.arange(leaves)[None, :] == request_ids[:, None], mid_of[None, :], 0), axis=1
    )
    root_ids = jnp.sum(
        jnp.where(jnp.arange(middles_all)[None, :] == middles[:, None], root_of[None, :], 0), axis=1
    )
    path_nodes = jnp.stack(
        [root_ids, roots_all + middles, roots_all + middles_all + request_ids], axis=1
    )
    picked = jnp.arange(nodes_all)[None, None, :] == path_nodes[:, :, None]
    lower_end = jnp.sum(jnp.where(picked, firsts[None, None, :], 0), axis=2)
    upper_end = lower_end + jnp.sum(jnp.where(picked, node_blocks[None, None, :], 0), axis=2)
    return (lower_end, upper_end)


def stage_kernel(n_pieces, own, number, first, last, base, *refs):
    refs = list(refs)
    count_ref, list_ref, mine_ref, theirs_ref = refs[:4]
    refs = refs[4:]
    if first:
        suffix_refs, refs = refs[:2], refs[2:]
    else:
        m_in, l_in, acc_in = refs[:3]
        refs = refs[3:]
    pieces, refs = refs[:n_pieces], refs[n_pieces:]
    if last:
        out_ref = refs.pop(0)
        m_ref, l_ref = m_in, l_in
    else:
        m_ref, l_ref, acc_out = refs[:3]
        refs = refs[3:]
    kv_ref, q_ref, acc_ref, piece_sems, q_sems, in_sems, out_sems = refs
    nreq, heads, rows, head_dim = q_ref.shape
    scale = head_dim ** (-0.5)
    stat = 0 if last else base

    def q_copy(j):
        source = (mine_ref, theirs_ref)[(base + j) % 2].at[(base + j) // 2]
        return pltpu.make_async_copy(source, q_ref.at[j], q_sems.at[j])

    def acc_copy(j):
        return pltpu.make_async_copy(acc_in.at[base + j], acc_ref.at[j], in_sems.at[j])

    def out_copy(j):
        return pltpu.make_async_copy(acc_ref.at[j], acc_out.at[base + j], out_sems.at[j])

    def piece_copy(i):
        return pltpu.make_async_copy(
            pieces[i], kv_ref.at[pl.ds(i * own, own)], piece_sems.at[i]
        )

    def active(j):
        return count_ref[number, base + j] > 0

    if first:
        for j in range(nreq):
            q_copy(j).start()
    for i in range(n_pieces):
        piece_copy(i).start()
    if not first:
        m_values, l_values = m_in[...], l_in[...]
        for j in range(nreq):

            @pl.when(active(j))
            def _():
                q_copy(j).start()
                acc_copy(j).start()

            if last:

                @pl.when(jnp.logical_not(active(j)))
                def _():
                    acc_copy(j).start()

        if not last:
            m_ref[...] = m_values
            l_ref[...] = l_values

    def dot(a, b):
        return jnp.dot(a, b, preferred_element_type=jnp.float32)

    def sweep(j, keys, values, old, mask=None):
        size = values.shape[0]
        values = jnp.concatenate([values.T, jnp.ones((16, size), jnp.bfloat16)], axis=0)
        scores, weights, tops, totals = {}, {}, [], []
        if old:
            highest, sums = m_ref[stat + j], l_ref[stat + j]
        for t in range(heads + 3):
            if t < heads:
                scores[t] = lax.dot_general(
                    keys, q_ref[j, t], (((1,), (1,)), ((), ())), preferred_element_type=jnp.float32
                )
            h = t - 3
            if h >= 0:
                p, factor = weights.pop(h)
                summed = dot(values, p)
                total = summed[head_dim : head_dim + 1]
                if old:
                    acc_ref[j, h] = acc_ref[j, h] * factor + summed[:head_dim]
                    total = sums[h : h + 1] * factor + total
                else:
                    acc_ref[j, h] = summed[:head_dim]
                totals.append(total)
            h = t - 2
            if 0 <= h < heads:
                s = scores.pop(h)
                if mask is not None:
                    s = jnp.where(mask, s, NEG)
                top = jnp.max(s, axis=0, keepdims=True)
                factor = None
                if old:
                    before = highest[h : h + 1]
                    top = jnp.maximum(before, top)
                    factor = jnp.exp((before - top) * scale)
                tops.append(top)
                p = jnp.exp((s - top).astype(jnp.bfloat16) * jnp.bfloat16(scale))
                weights[h] = (p, factor)
        m_ref[stat + j] = jnp.concatenate(tops, axis=0)
        l_ref[stat + j] = jnp.concatenate(totals, axis=0)

    if first:
        key_at = lax.broadcasted_iota(jnp.int32, (rows, rows), 0)
        row_at = lax.broadcasted_iota(jnp.int32, (rows, rows), 1)
        for j in range(nreq):
            q_copy(j).wait()
        for side in range(2):

            def start(k, carry, side=side):
                sfx = suffix_refs[side]
                sweep(2 * k + side, sfx[k, 0], sfx[k, 1], False, key_at <= row_at)
                return carry

            lax.fori_loop(0, nreq // 2, start, 0)

    for i in range(n_pieces):
        piece_copy(i).wait()

    def absorb(j, at, count):
        slots = [list_ref[number, base + j, at + u] for u in range(count)]
        keys = jnp.concatenate([kv_ref[s, 0] for s in slots], axis=0)
        values = jnp.concatenate([kv_ref[s, 1] for s in slots], axis=0)
        sweep(j, keys, values, True)

    for j in range(nreq):
        if not first:

            @pl.when(active(j))
            def _():
                q_copy(j).wait()
                acc_copy(j).wait()

            if last:

                @pl.when(jnp.logical_not(active(j)))
                def _():
                    acc_copy(j).wait()

    def request(j, carry):
        count = count_ref[number, base + j]
        groups = count // 8

        def eight(i, c):
            absorb(j, 8 * i, 8)
            return c

        lax.fori_loop(0, groups, eight, 0)
        for size in (4, 2, 1):

            @pl.when((count // size) % 2 == 1)
            def _():
                absorb(j, (count // (2 * size)) * (2 * size), size)

        return carry

    if pieces:
        lax.fori_loop(0, nreq, request, 0)

    if last:
        for j in range(nreq):
            for h in range(heads):
                done = acc_ref[j, h] * (1.0 / l_ref[j, pl.ds(h, 1), :])
                out_ref[:, h * head_dim : (h + 1) * head_dim] = done.astype(jnp.bfloat16).T
        return
    for j in range(nreq):
        if first:
            out_copy(j).start()
        else:

            @pl.when(active(j))
            def _():
                out_copy(j).start()

    for j in range(nreq):
        if first:
            out_copy(j).wait()
        else:

            @pl.when(active(j))
            def _():
                out_copy(j).wait()


SHORT = pl.CostEstimate(flops=1, bytes_accessed=1, transcendentals=0)
SMEM = pl.BlockSpec(memory_space=pltpu.SMEM)
VMEM = pl.BlockSpec(memory_space=pltpu.VMEM)
ANY = pl.BlockSpec(memory_space=pl.ANY)


def stage(number, work, queries, state, pieces, suffix=None, request=None, only=None):
    counts, lists = work
    half, heads, rows, head_dim = queries[0].shape
    own, _, block_tokens, _ = pieces[0].shape if pieces else (1, 2, 8, head_dim)
    first, last = suffix is not None, request is not None
    nreq = 1 if last else (only or 2 * half)
    base = request if last else 0
    scratch = [
        pltpu.VMEM((max(1, len(pieces)) * own, 2, block_tokens, head_dim), jnp.bfloat16),
        pltpu.VMEM((nreq, heads, rows, head_dim), jnp.bfloat16),
        pltpu.VMEM((nreq, heads, head_dim, rows), jnp.float32),
        pltpu.SemaphoreType.DMA((max(1, len(pieces)),)),
        pltpu.SemaphoreType.DMA((nreq,)),
        pltpu.SemaphoreType.DMA((nreq,)),
        pltpu.SemaphoreType.DMA((nreq,)),
    ]
    params = pltpu.CompilerParams(vmem_limit_bytes=48 * 1024 * 1024)
    body = functools.partial(stage_kernel, len(pieces), own, number, first, last, base)
    head_specs = [SMEM, SMEM, ANY, ANY]
    if last:
        stat = pl.BlockSpec((nreq, heads, rows), lambda i: (request, 0, 0))
        return pl.pallas_call(
            body,
            grid=(1,),
            in_specs=head_specs + [stat, stat, ANY] + [ANY] * len(pieces),
            out_specs=pl.BlockSpec((rows, heads * head_dim), lambda i: (0, 0)),
            out_shape=jax.ShapeDtypeStruct((rows, heads * head_dim), jnp.bfloat16),
            scratch_shapes=scratch,
            compiler_params=params,
            cost_estimate=SHORT,
        )(counts, lists, *queries, *state, *pieces)
    stats = jax.ShapeDtypeStruct((2 * half, heads, rows), jnp.float32)
    total = jax.ShapeDtypeStruct((2 * half, heads, head_dim, rows), jnp.float32)
    extra, extra_specs = (suffix, [VMEM] * 2) if first else (state, [VMEM, VMEM, ANY])
    return pl.pallas_call(
        body,
        in_specs=head_specs + extra_specs + [ANY] * len(pieces),
        out_specs=[VMEM, VMEM, ANY],
        out_shape=[stats, stats, total],
        scratch_shapes=scratch,
        compiler_params=params,
        cost_estimate=SHORT,
        input_output_aliases={} if first else {6: 2},
    )(counts, lists, *queries, *extra, *pieces)


def project_kernel(core_ref, mine_ref, theirs_ref, weight_ref, out_ref):
    depth = mine_ref.shape[1]
    core = core_ref[0]
    summed = jnp.dot(
        mine_ref[...],
        weight_ref[pl.ds(core * depth, depth), :],
        preferred_element_type=jnp.float32,
    ) + jnp.dot(
        theirs_ref[...],
        weight_ref[pl.ds((1 - core) * depth, depth), :],
        preferred_element_type=jnp.float32,
    )
    out_ref[...] = summed.astype(out_ref.dtype)


def project(core, mine, theirs, out_weight, part, parts, dtype):
    rows, depth = mine.shape
    columns = out_weight.shape[1] // parts
    width = min(512, columns)
    steps = columns // width
    whole = pl.BlockSpec((rows, depth), lambda i, c: (0, 0))
    return pl.pallas_call(
        project_kernel,
        grid_spec=pltpu.PrefetchScalarGridSpec(
            num_scalar_prefetch=1,
            grid=(steps,),
            in_specs=[
                whole,
                whole,
                pl.BlockSpec((out_weight.shape[0], width), lambda i, c: (0, part * steps + i)),
            ],
            out_specs=pl.BlockSpec((rows, width), lambda i, c: (0, i)),
        ),
        out_shape=jax.ShapeDtypeStruct((rows, columns), dtype),
        compiler_params=pltpu.CompilerParams(vmem_limit_bytes=48 * 1024 * 1024),
        cost_estimate=SHORT,
    )(core.reshape(1), mine, theirs, out_weight)


def ring_order(chips, at):
    half = chips // 2
    if chips == 8:
        place = jnp.where(at % 2 == 0, at // 2, chips - 1 - at // 2)
        chip = jnp.where(at < half, 2 * at, 2 * (chips - 1 - at) + 1)
    else:
        place = jnp.where(at < half, at, chips + half - 1 - at)
        chip = place
    return place, chip


def work_tables(plan, chips, own, group, lo, hi):
    most = max(len(pieces) for pieces in plan)
    filled = [pieces + [(0, -1)] * (most - len(pieces)) for pieces in plan]
    steps = jnp.asarray([[step for step, _ in pieces] for pieces in filled], jnp.int32)
    sides = jnp.asarray([[side for _, side in pieces] for pieces in filled], jnp.int32)
    place = ring_order(chips, group // CORES)[0]
    source = ring_order(chips, (place + steps + chips) % chips)[1]
    device = jnp.where(sides < 0, -chips * CORES, CORES * source + ((group % CORES) ^ sides))
    slots = jnp.arange(most * own)
    blocks = jnp.repeat(device * own, own, axis=1) + (slots % own)[None, :]
    inside = (blocks[:, None, None, :] >= lo[None, :, :, None]) & (
        blocks[:, None, None, :] < hi[None, :, :, None]
    )
    seen = jnp.any(inside, axis=2)
    ahead = slots[None, :] < slots[:, None]
    rank = jnp.sum(jnp.where(seen[:, :, None, :] & ahead, 1, 0), axis=3)
    here = seen[:, :, None, :] & (rank[:, :, None, :] == slots[:, None])
    lists = jnp.sum(jnp.where(here, slots, 0), axis=3)
    return jnp.sum(jnp.where(seen, 1, 0), axis=2).astype(jnp.int32), lists.astype(jnp.int32)


def on_device(chips, mems, queries, suffix_kv, prefix_kv, out_weight, node_blocks, root_of, mid_of):
    group = lax.axis_index("grp")
    mem = lax.axis_index("mem")
    core = group % CORES
    tokens_dev, heads_dev, head_dim = queries.shape
    reqs = tokens_dev // SUFFIX
    heads = heads_dev // CORES
    per_kv = QH // KVH
    own = prefix_kv.shape[0]
    half = chips // 2
    if chips == 8:
        ring = [0, 2, 4, 6, 7, 5, 3, 1]
    else:
        ring = list(range(half)) + list(range(half, chips))[::-1]

    swap = [(2 * s + c, 2 * s + 1 - c) for s in range(chips) for c in range(CORES)]
    ahead = [
        (2 * ring[i] + c, 2 * ring[(i + 1) % chips] + c) for i in range(chips) for c in range(CORES)
    ]
    behind = [(b, a) for a, b in ahead]

    kv_start = mem * heads_dev // per_kv
    kv_count = max(1, heads_dev // per_kv)

    def of_core(heads_kv, c):
        if kv_count == 1:
            return heads_kv[0]
        return jnp.where(c == 0, heads_kv[0], heads_kv[1])

    served = lax.dynamic_slice_in_dim(prefix_kv, kv_start, kv_count, 3)
    served = jnp.transpose(served, (3, 0, 1, 2, 4))
    own_a = of_core(served, core)
    own_b = lax.ppermute(of_core(served, 1 - core), "grp", swap)

    own_b, queries, suffix_kv, node_blocks, group = lax.optimization_barrier(
        (own_b, queries, suffix_kv, node_blocks, group)
    )

    order = (jnp.arange(reqs) + mem + 1) % reqs if mems == 2 else jnp.arange(reqs)

    def ordered(x):
        x = x.reshape((reqs, SUFFIX) + x.shape[1:])
        if mems != 2:
            return x
        return jnp.where(mem == 0, x[::-1], x)

    def query_part(c):
        return lax.dynamic_slice_in_dim(q_ordered, c * heads, heads, 1)

    q_ordered = jnp.transpose(ordered(queries), (0, 2, 1, 3))
    q = [query_part(core), lax.ppermute(query_part(1 - core), "grp", swap)]
    served = lax.dynamic_slice_in_dim(suffix_kv, kv_start, kv_count, 2)
    served = jnp.transpose(ordered(served), (3, 0, 2, 1, 4))
    suffix = [of_core(served, core), lax.ppermute(of_core(served, 1 - core), "grp", swap)]

    both = jnp.stack([group, group ^ 1])
    request_ids = (both[None, :] * reqs + order[:, None]).reshape(-1)
    lo, hi = path_ranges(request_ids, node_blocks, root_of, mid_of)
    far = chips // 2
    near = [[(-k, 0), (-k, 1), (k, 0), (k, 1)] for k in range(1, far)]
    final_plan = [(-far, 0), (far, 1)]
    work = work_tables(
        [[(0, 0), (0, 1)]] + near + [final_plan, near[-1] + final_plan], chips, own, group, lo, hi
    )

    def tied(x, y, state):
        return lax.optimization_barrier((x, y, state))

    state = stage(0, work, q, None, [], suffix=suffix)
    forth, back = [own_a, own_b], [own_a, own_b]
    for k in range(1, far):
        forth = [lax.ppermute(x, "grp", ahead) for x in forth]
        back = [lax.ppermute(x, "grp", behind) for x in back]
        if k == 1:
            forth[0], back[0], state = tied(forth[0], back[0], state)
            state = stage(0, work, q, state, [own_a, own_b])
        else:
            forth[0], back[0], state = tied(forth[0], back[0], state)
            state = stage(k - 1, work, q, state, last_step)
        forth[1], back[1], state = tied(forth[1], back[1], state)
        last_step = forth + back
    step = forth + back
    sent_state = stage(far - 1, work, q, state, step, only=reqs)
    final = [lax.ppermute(forth[0], "grp", ahead), lax.ppermute(back[1], "grp", behind)]

    def attended(part, state):
        if part == 0:
            number, pieces = far, final
        else:
            number, pieces = far + 1, step + final
        leaving = stage(number, work, q, state, pieces, request=2 * part + 1)
        staying = stage(number, work, q, state, pieces, request=2 * part)
        return staying, lax.ppermute(leaving, "grp", swap)

    if mems != 2:
        rows = [
            project(core, *attended(k, sent_state), out_weight, 0, 1, jnp.bfloat16)
            for k in range(reqs)
        ]
        return lax.psum_scatter(
            jnp.concatenate(rows, axis=0), "mem", scatter_dimension=0, tiled=True
        )
    parts = 2
    leaving, state = attended(0, sent_state), sent_state
    got = []
    for i in range(parts):
        sent = project(core, *leaving, out_weight, i, parts, jnp.bfloat16)
        sent, leaving, state = lax.optimization_barrier((sent, leaving, state))
        got.append(lax.ppermute(sent, "mem", [(0, 1), (1, 0)]))
    kept = lax.cond(
        node_blocks[0] >= 0,
        lambda now: project(core, *attended(1, now), out_weight, 0, 1, jnp.float32),
        lambda now: jnp.zeros((SUFFIX, out_weight.shape[1]), jnp.float32),
        state,
    )
    return (kept + jnp.concatenate(got, axis=1).astype(jnp.float32)).astype(jnp.bfloat16)


def solution(mesh):
    return jax.shard_map(
        functools.partial(on_device, mesh.shape["grp"] // CORES, mesh.shape["mem"]),
        mesh=mesh,
        in_specs=(
            P("grp", "mem", None),
            P("grp", None, None, None),
            P("grp", None, None, None, None),
            P("mem", None),
            P(),
            P(),
            P(),
        ),
        out_specs=P(("grp", "mem"), None),
        check_vma=False,
    )
```

```python
import functools

import jax
import jax.numpy as jnp
from jax import lax
from jax.experimental import pallas as pl
from jax.experimental.pallas import tpu as pltpu
from jax.sharding import PartitionSpec as P

QH = 32
KVH = 4
SUFFIX = 256
CORES = 2
NEG = -1e30


def path_ranges(request_ids, node_blocks, root_of, mid_of):
    nodes_all = node_blocks.shape[0]
    middles_all = root_of.shape[0]
    leaves = mid_of.shape[0]
    roots_all = nodes_all - middles_all - leaves
    firsts = jnp.cumsum(node_blocks) - node_blocks
    middles = jnp.sum(
        jnp.where(jnp.arange(leaves)[None, :] == request_ids[:, None], mid_of[None, :], 0), axis=1
    )
    root_ids = jnp.sum(
        jnp.where(jnp.arange(middles_all)[None, :] == middles[:, None], root_of[None, :], 0), axis=1
    )
    path_nodes = jnp.stack(
        [root_ids, roots_all + middles, roots_all + middles_all + request_ids], axis=1
    )
    picked = jnp.arange(nodes_all)[None, None, :] == path_nodes[:, :, None]
    lower_end = jnp.sum(jnp.where(picked, firsts[None, None, :], 0), axis=2)
    upper_end = lower_end + jnp.sum(jnp.where(picked, node_blocks[None, None, :], 0), axis=2)
    return (lower_end, upper_end)


def stage_kernel(n_pieces, own, number, first, last, base, *refs):
    refs = list(refs)
    count_ref, list_ref, mine_ref, theirs_ref = refs[:4]
    refs = refs[4:]
    if first:
        suffix_refs, refs = refs[:2], refs[2:]
    else:
        state_in, refs = refs[:3], refs[3:]
    pieces, refs = refs[:n_pieces], refs[n_pieces:]
    if last:
        out_refs, state_refs, refs = refs[:2], refs[2:5], refs[5:]
        for mine, given in zip(state_refs, state_in):
            mine[...] = given[base : base + mine.shape[0]]
        m_ref, l_ref, acc_ref = state_refs
    else:
        m_ref, l_ref, acc_ref = refs[:3]
        refs = refs[3:]
    kv_ref, q_ref, piece_sems, q_sems = refs
    nreq, heads, rows, head_dim = q_ref.shape
    scale = head_dim ** (-0.5)
    first_row = 0 if last else base

    def q_copy(j):
        source = (mine_ref, theirs_ref)[(base + j) % 2].at[(base + j) // 2]
        return pltpu.make_async_copy(source, q_ref.at[j], q_sems.at[j])

    def piece_copy(i):
        return pltpu.make_async_copy(
            pieces[i], kv_ref.at[pl.ds(i * own, own)], piece_sems.at[i]
        )

    def active(j):
        return count_ref[number, base + j] > 0

    if first:
        for j in range(nreq):
            q_copy(j).start()
    else:
        work = active(0)
        for j in range(1, nreq):
            work = work | active(j)

        @pl.when(work)
        def _():
            for i in range(n_pieces):
                piece_copy(i).start()

        for j in range(nreq):

            @pl.when(active(j))
            def _():
                q_copy(j).start()

    def dot(a, b):
        return jnp.dot(a, b, preferred_element_type=jnp.float32)

    def sweep(j, keys, values, old, mask=None):
        size = values.shape[0]
        values = jnp.concatenate([values.T, jnp.ones((16, size), jnp.bfloat16)], axis=0)
        scores, weights, tops, totals = {}, {}, [], []
        if old:
            highest, sums = m_ref[first_row + j], l_ref[first_row + j]
        for t in range(heads + 3):
            if t < heads:
                scores[t] = lax.dot_general(
                    keys, q_ref[j, t], (((1,), (1,)), ((), ())), preferred_element_type=jnp.float32
                )
            h = t - 3
            if h >= 0:
                p, factor = weights.pop(h)
                summed = dot(values, p)
                total = summed[head_dim : head_dim + 1]
                if old:
                    acc_ref[first_row + j, h] = acc_ref[first_row + j, h] * factor + summed[:head_dim]
                    total = sums[h : h + 1] * factor + total
                else:
                    acc_ref[first_row + j, h] = summed[:head_dim]
                totals.append(total)
            h = t - 2
            if 0 <= h < heads:
                s = scores.pop(h)
                if mask is not None:
                    s = jnp.where(mask, s, NEG)
                top = jnp.max(s, axis=0, keepdims=True)
                factor = None
                if old:
                    before = highest[h : h + 1]
                    top = jnp.maximum(before, top)
                    factor = jnp.exp((before - top) * scale)
                tops.append(top)
                p = jnp.exp((s - top).astype(jnp.bfloat16) * jnp.bfloat16(scale))
                weights[h] = (p, factor)
        m_ref[first_row + j] = jnp.concatenate(tops, axis=0)
        l_ref[first_row + j] = jnp.concatenate(totals, axis=0)

    if first:
        key_at = lax.broadcasted_iota(jnp.int32, (rows, rows), 0)
        row_at = lax.broadcasted_iota(jnp.int32, (rows, rows), 1)
        for j in range(nreq):
            q_copy(j).wait()
        for side in range(2):

            def start(k, carry, side=side):
                sfx = suffix_refs[side]
                sweep(2 * k + side, sfx[k, 0], sfx[k, 1], False, key_at <= row_at)
                return carry

            lax.fori_loop(0, nreq // 2, start, 0)

        return

    @pl.when(work)
    def _():
        for i in range(n_pieces):
            piece_copy(i).wait()

    def absorb(j, at, count):
        slots = [list_ref[number, base + j, at + u] for u in range(count)]
        keys = jnp.concatenate([kv_ref[s, 0] for s in slots], axis=0)
        values = jnp.concatenate([kv_ref[s, 1] for s in slots], axis=0)
        sweep(j, keys, values, True)

    for j in range(nreq):

        @pl.when(active(j))
        def _():
            q_copy(j).wait()

    def request(j, carry):
        count = count_ref[number, base + j]
        groups = count // 8

        def eight(i, c):
            absorb(j, 8 * i, 8)
            return c

        lax.fori_loop(0, groups, eight, 0)
        for size in (4, 2, 1):

            @pl.when((count // size) % 2 == 1)
            def _():
                absorb(j, (count // (2 * size)) * (2 * size), size)

        return carry

    lax.fori_loop(0, nreq, request, 0)

    if last:
        for j in range(nreq):
            for h in range(heads):
                done = acc_ref[first_row + j, h] * (1.0 / l_ref[first_row + j, pl.ds(h, 1), :])
                out_refs[j % 2][:, h * head_dim : (h + 1) * head_dim] = done.astype(jnp.bfloat16).T


SHORT = pl.CostEstimate(flops=1, bytes_accessed=1, transcendentals=0)
SCOPED = 28 * 1024 * 1024
SMEM = pl.BlockSpec(memory_space=pltpu.SMEM)
VMEM = pl.BlockSpec(memory_space=pltpu.VMEM)
ANY = pl.BlockSpec(memory_space=pl.ANY)


def stage(number, work, queries, state, pieces, suffix=None, base=0, nreq=None, last=False):
    counts, lists = work
    half, heads, rows, head_dim = queries[0].shape
    own, _, block_tokens, _ = pieces[0].shape if pieces else (1, 2, 8, head_dim)
    first = suffix is not None
    nreq = nreq or 2 * half
    held = [
        pltpu.VMEM((nreq, heads, rows), jnp.float32),
        pltpu.VMEM((nreq, heads, rows), jnp.float32),
        pltpu.VMEM((nreq, heads, head_dim, rows), jnp.float32),
    ]
    scratch = (held if last else []) + [
        pltpu.VMEM((max(1, len(pieces)) * own, 2, block_tokens, head_dim), jnp.bfloat16),
        pltpu.VMEM((nreq, heads, rows, head_dim), jnp.bfloat16),
        pltpu.SemaphoreType.DMA((max(1, len(pieces)),)),
        pltpu.SemaphoreType.DMA((nreq,)),
    ]
    stats = jax.ShapeDtypeStruct((2 * half, heads, rows), jnp.float32)
    total = jax.ShapeDtypeStruct((2 * half, heads, head_dim, rows), jnp.float32)
    done = jax.ShapeDtypeStruct((rows, heads * head_dim), jnp.bfloat16)
    extra = suffix if first else state
    return pl.pallas_call(
        functools.partial(stage_kernel, len(pieces), own, number, first, last, base),
        in_specs=[SMEM, SMEM, ANY, ANY] + [VMEM] * len(extra) + [ANY] * len(pieces),
        out_specs=[VMEM] * 2 if last else [VMEM] * 3,
        out_shape=[done] * 2 if last else [stats, stats, total],
        scratch_shapes=scratch,
        compiler_params=pltpu.CompilerParams(vmem_limit_bytes=SCOPED),
        cost_estimate=SHORT,
        input_output_aliases={} if first or last else {4: 0, 5: 1, 6: 2},
    )(counts, lists, *queries, *extra, *pieces)


def project_kernel(start, core_ref, mine_ref, theirs_ref, weight_ref, out_ref):
    depth = mine_ref.shape[1]
    core = core_ref[0]
    columns = out_ref.shape[1]
    width = min(512, columns)
    for at in range(0, columns, width):
        across = pl.ds(start + at, width)
        summed = jnp.dot(
            mine_ref[...],
            weight_ref[pl.ds(core * depth, depth), across],
            preferred_element_type=jnp.float32,
        ) + jnp.dot(
            theirs_ref[...],
            weight_ref[pl.ds((1 - core) * depth, depth), across],
            preferred_element_type=jnp.float32,
        )
        out_ref[:, at : at + width] = summed.astype(out_ref.dtype)


def project(core, mine, theirs, out_weight, part, parts, dtype):
    columns = out_weight.shape[1] // parts
    return pl.pallas_call(
        functools.partial(project_kernel, part * columns),
        in_specs=[SMEM, VMEM, VMEM, VMEM],
        out_specs=VMEM,
        out_shape=jax.ShapeDtypeStruct((mine.shape[0], columns), dtype),
        compiler_params=pltpu.CompilerParams(vmem_limit_bytes=SCOPED),
        cost_estimate=SHORT,
    )(core.reshape(1), mine, theirs, out_weight)


def ring_order(chips, at):
    half = chips // 2
    if chips == 8:
        place = jnp.where(at % 2 == 0, at // 2, chips - 1 - at // 2)
        chip = jnp.where(at < half, 2 * at, 2 * (chips - 1 - at) + 1)
    else:
        place = jnp.where(at < half, at, chips + half - 1 - at)
        chip = place
    return place, chip


def work_tables(plan, chips, own, group, lo, hi):
    most = max(len(pieces) for pieces in plan)
    filled = [pieces + [(0, -1)] * (most - len(pieces)) for pieces in plan]
    steps = jnp.asarray([[step for step, _ in pieces] for pieces in filled], jnp.int32)
    sides = jnp.asarray([[side for _, side in pieces] for pieces in filled], jnp.int32)
    place = ring_order(chips, group // CORES)[0]
    source = ring_order(chips, (place + steps + chips) % chips)[1]
    device = jnp.where(sides < 0, -chips * CORES, CORES * source + ((group % CORES) ^ sides))
    slots = jnp.arange(most * own)
    blocks = jnp.repeat(device * own, own, axis=1) + (slots % own)[None, :]
    inside = (blocks[:, None, None, :] >= lo[None, :, :, None]) & (
        blocks[:, None, None, :] < hi[None, :, :, None]
    )
    seen = jnp.any(inside, axis=2)
    ahead = slots[None, :] < slots[:, None]
    rank = jnp.sum(jnp.where(seen[:, :, None, :] & ahead, 1, 0), axis=3)
    here = seen[:, :, None, :] & (rank[:, :, None, :] == slots[:, None])
    lists = jnp.sum(jnp.where(here, slots, 0), axis=3)
    return jnp.sum(jnp.where(seen, 1, 0), axis=2).astype(jnp.int32), lists.astype(jnp.int32)


def on_device(chips, mems, queries, suffix_kv, prefix_kv, out_weight, node_blocks, root_of, mid_of):
    group = lax.axis_index("grp")
    mem = lax.axis_index("mem")
    core = group % CORES
    tokens_dev, heads_dev, head_dim = queries.shape
    reqs = tokens_dev // SUFFIX
    heads = heads_dev // CORES
    per_kv = QH // KVH
    own = prefix_kv.shape[0]
    half = chips // 2
    if chips == 8:
        ring = [0, 2, 4, 6, 7, 5, 3, 1]
    else:
        ring = list(range(half)) + list(range(half, chips))[::-1]

    swap = [(2 * s + c, 2 * s + 1 - c) for s in range(chips) for c in range(CORES)]
    ahead = [
        (2 * ring[i] + c, 2 * ring[(i + 1) % chips] + c) for i in range(chips) for c in range(CORES)
    ]
    behind = [(b, a) for a, b in ahead]

    kv_start = mem * heads_dev // per_kv
    kv_count = max(1, heads_dev // per_kv)

    def of_core(heads_kv, c):
        if kv_count == 1:
            return heads_kv[0]
        return jnp.where(c == 0, heads_kv[0], heads_kv[1])

    served = lax.dynamic_slice_in_dim(prefix_kv, kv_start, kv_count, 3)
    served = jnp.transpose(served, (3, 0, 1, 2, 4))
    own_a = of_core(served, core)
    own_b = lax.ppermute(of_core(served, 1 - core), "grp", swap)

    own_b, queries, suffix_kv, node_blocks, group = lax.optimization_barrier(
        (own_b, queries, suffix_kv, node_blocks, group)
    )

    order = (jnp.arange(reqs) + mem + 1) % reqs if mems == 2 else jnp.arange(reqs)

    def ordered(x):
        x = x.reshape((reqs, SUFFIX) + x.shape[1:])
        if mems != 2:
            return x
        return jnp.where(mem == 0, x[::-1], x)

    def query_part(c):
        return lax.dynamic_slice_in_dim(q_ordered, c * heads, heads, 1)

    q_ordered = jnp.transpose(ordered(queries), (0, 2, 1, 3))
    q = [query_part(core), lax.ppermute(query_part(1 - core), "grp", swap)]
    served = lax.dynamic_slice_in_dim(suffix_kv, kv_start, kv_count, 2)
    served = jnp.transpose(ordered(served), (3, 0, 2, 1, 4))
    suffix = [of_core(served, core), lax.ppermute(of_core(served, 1 - core), "grp", swap)]

    both = jnp.stack([group, group ^ 1])
    request_ids = (both[None, :] * reqs + order[:, None]).reshape(-1)
    lo, hi = path_ranges(request_ids, node_blocks, root_of, mid_of)
    far = chips // 2
    near = [[(-k, 0), (-k, 1), (k, 0), (k, 1)] for k in range(1, far)]
    final_plan = [(-far, 0), (far, 1)]
    work = work_tables(
        [[(0, 0), (0, 1)]] + near + [final_plan, near[-1] + final_plan], chips, own, group, lo, hi
    )

    def tied(x, y, state):
        return lax.optimization_barrier((x, y, state))

    state = stage(0, work, q, None, [], suffix=suffix)
    forth, back = [own_a, own_b], [own_a, own_b]
    for k in range(1, far):
        forth = [lax.ppermute(x, "grp", ahead) for x in forth]
        back = [lax.ppermute(x, "grp", behind) for x in back]
        if k == 1:
            forth[0], back[0], state = tied(forth[0], back[0], state)
            state = stage(0, work, q, state, [own_a, own_b])
        else:
            forth[0], back[0], state = tied(forth[0], back[0], state)
            state = stage(k - 1, work, q, state, last_step)
        forth[1], back[1], state = tied(forth[1], back[1], state)
        last_step = forth + back
    step = forth + back
    state = stage(far - 1, work, q, state, step, nreq=reqs)
    final = [lax.ppermute(forth[0], "grp", ahead), lax.ppermute(back[1], "grp", behind)]

    def attended(part, state):
        number, pieces = (far, final) if part == 0 else (far + 1, step + final)
        staying, leaving = stage(
            number, work, q, state, pieces, base=2 * part, nreq=2, last=True
        )
        return staying, lax.ppermute(leaving, "grp", swap)

    if mems != 2:
        rows = [
            project(core, *attended(k, state), out_weight, 0, 1, jnp.bfloat16) for k in range(reqs)
        ]
        return lax.psum_scatter(
            jnp.concatenate(rows, axis=0), "mem", scatter_dimension=0, tiled=True
        )

    def exchange(x):
        return lax.ppermute(x, "mem", [(0, 1), (1, 0)])

    def part_of(rows, i, dtype):
        return project(core, *rows, out_weight, i, 2, dtype)

    def follows(work_now, *now):
        shapes = jax.eval_shape(work_now, *now)
        return lax.cond(
            node_blocks[0] >= 0,
            work_now,
            lambda *_: jax.tree.map(lambda x: jnp.zeros(x.shape, x.dtype), shapes),
            *now,
        )

    def keep(state):
        rows = attended(1, state)
        return [part_of(rows, i, jnp.float32) for i in range(2)]

    def second(rows, state):
        sent, state = lax.optimization_barrier((part_of(rows, 1, jnp.bfloat16), state))
        got = exchange(sent)
        kept = follows(keep, state)
        return got, kept

    rows = attended(0, state)
    sent, rows, state = lax.optimization_barrier((part_of(rows, 0, jnp.bfloat16), rows, state))
    got = [exchange(sent)]
    late, kept = follows(second, rows, state)
    got.append(late)
    return jnp.concatenate(
        [(k + g.astype(jnp.float32)).astype(jnp.bfloat16) for k, g in zip(kept, got)], axis=1
    )


def solution(mesh):
    return jax.shard_map(
        functools.partial(on_device, mesh.shape["grp"] // CORES, mesh.shape["mem"]),
        mesh=mesh,
        in_specs=(
            P("grp", "mem", None),
            P("grp", None, None, None),
            P("grp", None, None, None, None),
            P("mem", None),
            P(),
            P(),
            P(),
        ),
        out_specs=P(("grp", "mem"), None),
        check_vma=False,
    )
```

```python
import functools

import jax
import jax.numpy as jnp
from jax import lax
from jax.experimental import pallas as pl
from jax.experimental.pallas import tpu as pltpu
from jax.sharding import PartitionSpec as P

QH = 32
KVH = 4
SUFFIX = 256
CORES = 2
NEG = -1e30


def path_ranges(request_ids, node_blocks, root_of, mid_of):
    nodes_all = node_blocks.shape[0]
    middles_all = root_of.shape[0]
    leaves = mid_of.shape[0]
    roots_all = nodes_all - middles_all - leaves
    firsts = jnp.cumsum(node_blocks) - node_blocks
    middles = jnp.sum(
        jnp.where(jnp.arange(leaves)[None, :] == request_ids[:, None], mid_of[None, :], 0), axis=1
    )
    root_ids = jnp.sum(
        jnp.where(jnp.arange(middles_all)[None, :] == middles[:, None], root_of[None, :], 0), axis=1
    )
    path_nodes = jnp.stack(
        [root_ids, roots_all + middles, roots_all + middles_all + request_ids], axis=1
    )
    picked = jnp.arange(nodes_all)[None, None, :] == path_nodes[:, :, None]
    lower_end = jnp.sum(jnp.where(picked, firsts[None, None, :], 0), axis=2)
    upper_end = lower_end + jnp.sum(jnp.where(picked, node_blocks[None, None, :], 0), axis=2)
    return (lower_end, upper_end)


def stage_kernel(n_pieces, own, number, first, last, base, *refs):
    refs = list(refs)
    count_ref, list_ref, mine_ref, theirs_ref = refs[:4]
    refs = refs[4:]
    if first:
        suffix_refs, refs = refs[:2], refs[2:]
    else:
        state_in, refs = refs[:3], refs[3:]
    pieces, refs = refs[:n_pieces], refs[n_pieces:]
    if last:
        out_refs, state_refs, refs = refs[:2], refs[2:5], refs[5:]
        for mine, given in zip(state_refs, state_in):
            mine[...] = given[base : base + mine.shape[0]]
        m_ref, l_ref, acc_ref = state_refs
    else:
        m_ref, l_ref, acc_ref = refs[:3]
        refs = refs[3:]
    kv_ref, q_ref, piece_sems, q_sems = refs
    nreq, heads, rows, head_dim = q_ref.shape
    scale = head_dim ** (-0.5)
    first_row = 0 if last else base

    def q_copy(j):
        source = (mine_ref, theirs_ref)[(base + j) % 2].at[(base + j) // 2]
        return pltpu.make_async_copy(source, q_ref.at[j], q_sems.at[j])

    def piece_copy(i):
        return pltpu.make_async_copy(
            pieces[i], kv_ref.at[pl.ds(i * own, own)], piece_sems.at[i]
        )

    def active(j):
        return count_ref[number, base + j] > 0

    if first:
        for j in range(nreq):
            q_copy(j).start()
    else:
        work = active(0)
        for j in range(1, nreq):
            work = work | active(j)

        @pl.when(work)
        def _():
            for i in range(n_pieces):
                piece_copy(i).start()

        for j in range(nreq):

            @pl.when(active(j))
            def _():
                q_copy(j).start()

    def dot(a, b):
        return jnp.dot(a, b, preferred_element_type=jnp.float32)

    def sweep(j, keys, values, old, mask=None):
        size = values.shape[0]
        values = jnp.concatenate([values.T, jnp.ones((16, size), jnp.bfloat16)], axis=0)
        scores, weights, tops, totals = {}, {}, [], []
        if old:
            highest, sums = m_ref[first_row + j], l_ref[first_row + j]
        for t in range(heads + 3):
            if t < heads:
                scores[t] = lax.dot_general(
                    keys, q_ref[j, t], (((1,), (1,)), ((), ())), preferred_element_type=jnp.float32
                )
            h = t - 3
            if h >= 0:
                p, factor = weights.pop(h)
                summed = dot(values, p)
                total = summed[head_dim : head_dim + 1]
                if old:
                    acc_ref[first_row + j, h] = acc_ref[first_row + j, h] * factor + summed[:head_dim]
                    total = sums[h : h + 1] * factor + total
                else:
                    acc_ref[first_row + j, h] = summed[:head_dim]
                totals.append(total)
            h = t - 2
            if 0 <= h < heads:
                s = scores.pop(h)
                if mask is not None:
                    s = jnp.where(mask, s, NEG)
                top = jnp.max(s, axis=0, keepdims=True)
                factor = None
                if old:
                    before = highest[h : h + 1]
                    top = jnp.maximum(before, top)
                    factor = jnp.exp((before - top) * scale)
                tops.append(top)
                p = jnp.exp((s - top).astype(jnp.bfloat16) * jnp.bfloat16(scale))
                weights[h] = (p, factor)
        m_ref[first_row + j] = jnp.concatenate(tops, axis=0)
        l_ref[first_row + j] = jnp.concatenate(totals, axis=0)

    if first:
        key_at = lax.broadcasted_iota(jnp.int32, (rows, rows), 0)
        row_at = lax.broadcasted_iota(jnp.int32, (rows, rows), 1)
        for j in range(nreq):
            q_copy(j).wait()
        for side in range(2):

            def start(k, carry, side=side):
                sfx = suffix_refs[side]
                sweep(2 * k + side, sfx[k, 0], sfx[k, 1], False, key_at <= row_at)
                return carry

            lax.fori_loop(0, nreq // 2, start, 0)

        return

    @pl.when(work)
    def _():
        for i in range(n_pieces):
            piece_copy(i).wait()

    def absorb(j, at, count):
        slots = [list_ref[number, base + j, at + u] for u in range(count)]
        keys = jnp.concatenate([kv_ref[s, 0] for s in slots], axis=0)
        values = jnp.concatenate([kv_ref[s, 1] for s in slots], axis=0)
        sweep(j, keys, values, True)

    for j in range(nreq):

        @pl.when(active(j))
        def _():
            q_copy(j).wait()

    def request(j, carry):
        count = count_ref[number, base + j]
        groups = count // 8

        def eight(i, c):
            absorb(j, 8 * i, 8)
            return c

        lax.fori_loop(0, groups, eight, 0)
        for size in (4, 2, 1):

            @pl.when((count // size) % 2 == 1)
            def _():
                absorb(j, (count // (2 * size)) * (2 * size), size)

        return carry

    lax.fori_loop(0, nreq, request, 0)

    if last:
        for j in range(nreq):
            for h in range(heads):
                done = acc_ref[first_row + j, h] * (1.0 / l_ref[first_row + j, pl.ds(h, 1), :])
                out_refs[j % 2][:, h * head_dim : (h + 1) * head_dim] = done.astype(jnp.bfloat16).T


SHORT = pl.CostEstimate(flops=1, bytes_accessed=1, transcendentals=0)
SCOPED = 28 * 1024 * 1024
SMEM = pl.BlockSpec(memory_space=pltpu.SMEM)
VMEM = pl.BlockSpec(memory_space=pltpu.VMEM)
ANY = pl.BlockSpec(memory_space=pl.ANY)


def stage(number, work, queries, state, pieces, suffix=None, base=0, nreq=None, last=False):
    counts, lists = work
    half, heads, rows, head_dim = queries[0].shape
    own, _, block_tokens, _ = pieces[0].shape if pieces else (1, 2, 8, head_dim)
    first = suffix is not None
    nreq = nreq or 2 * half
    held = [
        pltpu.VMEM((nreq, heads, rows), jnp.float32),
        pltpu.VMEM((nreq, heads, rows), jnp.float32),
        pltpu.VMEM((nreq, heads, head_dim, rows), jnp.float32),
    ]
    scratch = (held if last else []) + [
        pltpu.VMEM((max(1, len(pieces)) * own, 2, block_tokens, head_dim), jnp.bfloat16),
        pltpu.VMEM((nreq, heads, rows, head_dim), jnp.bfloat16),
        pltpu.SemaphoreType.DMA((max(1, len(pieces)),)),
        pltpu.SemaphoreType.DMA((nreq,)),
    ]
    stats = jax.ShapeDtypeStruct((2 * half, heads, rows), jnp.float32)
    total = jax.ShapeDtypeStruct((2 * half, heads, head_dim, rows), jnp.float32)
    done = jax.ShapeDtypeStruct((rows, heads * head_dim), jnp.bfloat16)
    extra = suffix if first else state
    return pl.pallas_call(
        functools.partial(stage_kernel, len(pieces), own, number, first, last, base),
        in_specs=[SMEM, SMEM, ANY, ANY] + [VMEM] * len(extra) + [ANY] * len(pieces),
        out_specs=[VMEM] * 2 if last else [VMEM] * 3,
        out_shape=[done] * 2 if last else [stats, stats, total],
        scratch_shapes=scratch,
        compiler_params=pltpu.CompilerParams(vmem_limit_bytes=SCOPED),
        cost_estimate=SHORT,
        input_output_aliases={} if first or last else {4: 0, 5: 1, 6: 2},
    )(counts, lists, *queries, *extra, *pieces)


def project_kernel(start, core_ref, mine_ref, theirs_ref, weight_ref, out_ref):
    depth = mine_ref.shape[1]
    core = core_ref[0]
    columns = out_ref.shape[1]
    width = min(512, columns)
    for at in range(0, columns, width):
        across = pl.ds(start + at, width)
        summed = jnp.dot(
            mine_ref[...],
            weight_ref[pl.ds(core * depth, depth), across],
            preferred_element_type=jnp.float32,
        ) + jnp.dot(
            theirs_ref[...],
            weight_ref[pl.ds((1 - core) * depth, depth), across],
            preferred_element_type=jnp.float32,
        )
        out_ref[:, at : at + width] = summed.astype(out_ref.dtype)


def project(core, mine, theirs, out_weight, part, parts, dtype):
    columns = out_weight.shape[1] // parts
    return pl.pallas_call(
        functools.partial(project_kernel, part * columns),
        in_specs=[SMEM, VMEM, VMEM, VMEM],
        out_specs=VMEM,
        out_shape=jax.ShapeDtypeStruct((mine.shape[0], columns), dtype),
        compiler_params=pltpu.CompilerParams(vmem_limit_bytes=SCOPED),
        cost_estimate=SHORT,
    )(core.reshape(1), mine, theirs, out_weight)


def add_kernel(*refs):
    out_ref = refs[-1]
    count = (len(refs) - 1) // 2
    for i in range(count):
        kept, got = refs[i], refs[count + i]
        width = kept.shape[1]
        out_ref[:, i * width : (i + 1) * width] = (
            kept[...] + got[...].astype(jnp.float32)
        ).astype(out_ref.dtype)


def add(kept, got):
    rows, width = kept[0].shape
    return pl.pallas_call(
        add_kernel,
        in_specs=[VMEM] * (2 * len(kept)),
        out_specs=VMEM,
        out_shape=jax.ShapeDtypeStruct((rows, width * len(kept)), jnp.bfloat16),
        compiler_params=pltpu.CompilerParams(vmem_limit_bytes=SCOPED),
        cost_estimate=SHORT,
    )(*kept, *got)


def ring_order(chips, at):
    half = chips // 2
    if chips == 8:
        place = jnp.where(at % 2 == 0, at // 2, chips - 1 - at // 2)
        chip = jnp.where(at < half, 2 * at, 2 * (chips - 1 - at) + 1)
    else:
        place = jnp.where(at < half, at, chips + half - 1 - at)
        chip = place
    return place, chip


def work_tables(plan, chips, own, group, lo, hi):
    most = max(len(pieces) for pieces in plan)
    filled = [pieces + [(0, -1)] * (most - len(pieces)) for pieces in plan]
    steps = jnp.asarray([[step for step, _ in pieces] for pieces in filled], jnp.int32)
    sides = jnp.asarray([[side for _, side in pieces] for pieces in filled], jnp.int32)
    place = ring_order(chips, group // CORES)[0]
    source = ring_order(chips, (place + steps + chips) % chips)[1]
    device = jnp.where(sides < 0, -chips * CORES, CORES * source + ((group % CORES) ^ sides))
    slots = jnp.arange(most * own)
    blocks = jnp.repeat(device * own, own, axis=1) + (slots % own)[None, :]
    inside = (blocks[:, None, None, :] >= lo[None, :, :, None]) & (
        blocks[:, None, None, :] < hi[None, :, :, None]
    )
    seen = jnp.any(inside, axis=2)
    ahead = slots[None, :] < slots[:, None]
    rank = jnp.sum(jnp.where(seen[:, :, None, :] & ahead, 1, 0), axis=3)
    here = seen[:, :, None, :] & (rank[:, :, None, :] == slots[:, None])
    lists = jnp.sum(jnp.where(here, slots, 0), axis=3)
    return jnp.sum(jnp.where(seen, 1, 0), axis=2).astype(jnp.int32), lists.astype(jnp.int32)


def on_device(chips, mems, queries, suffix_kv, prefix_kv, out_weight, node_blocks, root_of, mid_of):
    group = lax.axis_index("grp")
    mem = lax.axis_index("mem")
    core = group % CORES
    tokens_dev, heads_dev, head_dim = queries.shape
    reqs = tokens_dev // SUFFIX
    heads = heads_dev // CORES
    per_kv = QH // KVH
    own = prefix_kv.shape[0]
    half = chips // 2
    if chips == 8:
        ring = [0, 2, 4, 6, 7, 5, 3, 1]
    else:
        ring = list(range(half)) + list(range(half, chips))[::-1]

    swap = [(2 * s + c, 2 * s + 1 - c) for s in range(chips) for c in range(CORES)]
    ahead = [
        (2 * ring[i] + c, 2 * ring[(i + 1) % chips] + c) for i in range(chips) for c in range(CORES)
    ]
    behind = [(b, a) for a, b in ahead]

    kv_start = mem * heads_dev // per_kv
    kv_count = max(1, heads_dev // per_kv)

    def of_core(heads_kv, c):
        if kv_count == 1:
            return heads_kv[0]
        return jnp.where(c == 0, heads_kv[0], heads_kv[1])

    served = lax.dynamic_slice_in_dim(prefix_kv, kv_start, kv_count, 3)
    served = jnp.transpose(served, (3, 0, 1, 2, 4))
    own_a = of_core(served, core)
    own_b = lax.ppermute(of_core(served, 1 - core), "grp", swap)

    own_b, queries, suffix_kv, node_blocks, group = lax.optimization_barrier(
        (own_b, queries, suffix_kv, node_blocks, group)
    )

    order = (jnp.arange(reqs) + mem + 1) % reqs if mems == 2 else jnp.arange(reqs)

    def ordered(x):
        x = x.reshape((reqs, SUFFIX) + x.shape[1:])
        if mems != 2:
            return x
        return jnp.where(mem == 0, x[::-1], x)

    def query_part(c):
        return lax.dynamic_slice_in_dim(q_ordered, c * heads, heads, 1)

    q_ordered = jnp.transpose(ordered(queries), (0, 2, 1, 3))
    q = [query_part(core), lax.ppermute(query_part(1 - core), "grp", swap)]
    served = lax.dynamic_slice_in_dim(suffix_kv, kv_start, kv_count, 2)
    served = jnp.transpose(ordered(served), (3, 0, 2, 1, 4))
    suffix = [of_core(served, core), lax.ppermute(of_core(served, 1 - core), "grp", swap)]

    both = jnp.stack([group, group ^ 1])
    request_ids = (both[None, :] * reqs + order[:, None]).reshape(-1)
    lo, hi = path_ranges(request_ids, node_blocks, root_of, mid_of)
    far = chips // 2
    near = [[(-k, 0), (-k, 1), (k, 0), (k, 1)] for k in range(1, far)]
    final_plan = [(-far, 0), (far, 1)]
    work = work_tables(
        [[(0, 0), (0, 1)]] + near + [final_plan, near[-2] + near[-1] + final_plan],
        chips,
        own,
        group,
        lo,
        hi,
    )

    def tied(x, y, state):
        return lax.optimization_barrier((x, y, state))

    state = stage(0, work, q, None, [], suffix=suffix)
    forth, back = [own_a, own_b], [own_a, own_b]
    for k in range(1, far):
        forth = [lax.ppermute(x, "grp", ahead) for x in forth]
        back = [lax.ppermute(x, "grp", behind) for x in back]
        if k == 1:
            forth[0], back[0], state = tied(forth[0], back[0], state)
            state = stage(0, work, q, state, [own_a, own_b])
        else:
            forth[0], back[0], state = tied(forth[0], back[0], state)
            late = k == far - 1
            state = stage(k - 1, work, q, state, last_step, nreq=reqs if late else None)
            before_last = last_step
        forth[1], back[1], state = tied(forth[1], back[1], state)
        last_step = forth + back
    step = forth + back
    state = stage(far - 1, work, q, state, step, nreq=reqs)
    final = [lax.ppermute(forth[0], "grp", ahead), lax.ppermute(back[1], "grp", behind)]

    def attended(part, state):
        number, pieces = (far, final) if part == 0 else (far + 1, before_last + step + final)
        staying, leaving = stage(
            number, work, q, state, pieces, base=2 * part, nreq=2, last=True
        )
        return staying, lax.ppermute(leaving, "grp", swap)

    if mems != 2:
        rows = [
            project(core, *attended(k, state), out_weight, 0, 1, jnp.bfloat16) for k in range(reqs)
        ]
        return lax.psum_scatter(
            jnp.concatenate(rows, axis=0), "mem", scatter_dimension=0, tiled=True
        )

    def exchange(x):
        return lax.ppermute(x, "mem", [(0, 1), (1, 0)])

    def part_of(rows, i, dtype):
        return project(core, *rows, out_weight, i, 2, dtype)

    def follows(work_now, *now):
        shapes = jax.eval_shape(work_now, *now)
        return lax.cond(
            node_blocks[0] >= 0,
            work_now,
            lambda *_: jax.tree.map(lambda x: jnp.zeros(x.shape, x.dtype), shapes),
            *now,
        )

    def keep(state):
        rows = attended(1, state)
        return [part_of(rows, i, jnp.float32) for i in range(2)]

    def second(rows, state):
        sent, state = lax.optimization_barrier((part_of(rows, 1, jnp.bfloat16), state))
        got = exchange(sent)
        kept = follows(keep, state)
        return got, kept

    rows = attended(0, state)
    sent, rows, state = lax.optimization_barrier((part_of(rows, 0, jnp.bfloat16), rows, state))
    got = [exchange(sent)]
    late, kept = follows(second, rows, state)
    got.append(late)
    return add(kept, got)


def solution(mesh):
    return jax.shard_map(
        functools.partial(on_device, mesh.shape["grp"] // CORES, mesh.shape["mem"]),
        mesh=mesh,
        in_specs=(
            P("grp", "mem", None),
            P("grp", None, None, None),
            P("grp", None, None, None, None),
            P("mem", None),
            P(),
            P(),
            P(),
        ),
        out_specs=P(("grp", "mem"), None),
        check_vma=False,
    )
```

```python
import functools

import jax
import jax.numpy as jnp
from jax import lax
from jax.experimental import pallas as pl
from jax.experimental.pallas import tpu as pltpu
from jax.sharding import PartitionSpec as P

QH = 32
KVH = 4
SUFFIX = 256
CORES = 2
NEG = -1e30


def path_ranges(request_ids, node_blocks, root_of, mid_of):
    nodes_all = node_blocks.shape[0]
    middles_all = root_of.shape[0]
    leaves = mid_of.shape[0]
    roots_all = nodes_all - middles_all - leaves
    firsts = jnp.cumsum(node_blocks) - node_blocks
    middles = jnp.sum(
        jnp.where(jnp.arange(leaves)[None, :] == request_ids[:, None], mid_of[None, :], 0), axis=1
    )
    root_ids = jnp.sum(
        jnp.where(jnp.arange(middles_all)[None, :] == middles[:, None], root_of[None, :], 0), axis=1
    )
    path_nodes = jnp.stack(
        [root_ids, roots_all + middles, roots_all + middles_all + request_ids], axis=1
    )
    picked = jnp.arange(nodes_all)[None, None, :] == path_nodes[:, :, None]
    lower_end = jnp.sum(jnp.where(picked, firsts[None, None, :], 0), axis=2)
    upper_end = lower_end + jnp.sum(jnp.where(picked, node_blocks[None, None, :], 0), axis=2)
    return (lower_end, upper_end)


def stage_kernel(n_pieces, own, number, first, last, base, *refs):
    refs = list(refs)
    count_ref, list_ref, mine_ref, theirs_ref = refs[:4]
    refs = refs[4:]
    if first:
        suffix_refs, refs = refs[:2], refs[2:]
    else:
        state_in, refs = refs[:3], refs[3:]
    pieces, refs = refs[:n_pieces], refs[n_pieces:]
    if last:
        out_refs, state_refs, refs = refs[:2], refs[2:5], refs[5:]
        m_ref, l_ref, acc_ref = state_refs
    else:
        m_ref, l_ref, acc_ref = refs[:3]
        refs = refs[3:]
    kv_ref, q_ref, piece_sems, q_sems = refs
    nreq, heads, rows, head_dim = q_ref.shape
    scale = head_dim ** (-0.5)
    first_row = 0 if last else base

    def q_copy(j):
        source = (mine_ref, theirs_ref)[(base + j) % 2].at[(base + j) // 2]
        return pltpu.make_async_copy(source, q_ref.at[j], q_sems.at[j])

    def piece_copy(i):
        return pltpu.make_async_copy(
            pieces[i], kv_ref.at[pl.ds(i * own, own)], piece_sems.at[i]
        )

    def active(j):
        return count_ref[number, base + j] > 0

    if first:
        for j in range(nreq):
            q_copy(j).start()
    else:
        work = active(0)
        for j in range(1, nreq):
            work = work | active(j)

        @pl.when(work)
        def _():
            for i in range(n_pieces):
                piece_copy(i).start()

        for j in range(nreq):

            @pl.when(active(j))
            def _():
                q_copy(j).start()
                if last:
                    for mine, given in zip(state_refs, state_in):
                        mine[j] = given[base + j]

    def dot(a, b):
        return jnp.dot(a, b, preferred_element_type=jnp.float32)

    def sweep(j, keys, values, old, mask=None):
        size = values.shape[0]
        values = jnp.concatenate([values.T, jnp.ones((16, size), jnp.bfloat16)], axis=0)
        scores, weights, tops, totals = {}, {}, [], []
        if old:
            highest, sums = m_ref[first_row + j], l_ref[first_row + j]
        for t in range(heads + 3):
            if t < heads:
                scores[t] = lax.dot_general(
                    keys, q_ref[j, t], (((1,), (1,)), ((), ())), preferred_element_type=jnp.float32
                )
            h = t - 3
            if h >= 0:
                p, factor = weights.pop(h)
                summed = dot(values, p)
                total = summed[head_dim : head_dim + 1]
                if old:
                    acc_ref[first_row + j, h] = acc_ref[first_row + j, h] * factor + summed[:head_dim]
                    total = sums[h : h + 1] * factor + total
                else:
                    acc_ref[first_row + j, h] = summed[:head_dim]
                totals.append(total)
            h = t - 2
            if 0 <= h < heads:
                s = scores.pop(h)
                if mask is not None:
                    s = jnp.where(mask, s, NEG)
                top = jnp.max(s, axis=0, keepdims=True)
                factor = None
                if old:
                    before = highest[h : h + 1]
                    top = jnp.maximum(before, top)
                    factor = jnp.exp((before - top) * scale)
                tops.append(top)
                p = jnp.exp((s - top).astype(jnp.bfloat16) * jnp.bfloat16(scale))
                weights[h] = (p, factor)
        m_ref[first_row + j] = jnp.concatenate(tops, axis=0)
        l_ref[first_row + j] = jnp.concatenate(totals, axis=0)

    if first:
        key_at = lax.broadcasted_iota(jnp.int32, (rows, rows), 0)
        row_at = lax.broadcasted_iota(jnp.int32, (rows, rows), 1)
        for j in range(nreq):
            q_copy(j).wait()
        for side in range(2):

            def start(k, carry, side=side):
                sfx = suffix_refs[side]
                sweep(2 * k + side, sfx[k, 0], sfx[k, 1], False, key_at <= row_at)
                return carry

            lax.fori_loop(0, nreq // 2, start, 0)

        return

    @pl.when(work)
    def _():
        for i in range(n_pieces):
            piece_copy(i).wait()

    def absorb(j, at, count):
        slots = [list_ref[number, base + j, at + u] for u in range(count)]
        keys = jnp.concatenate([kv_ref[s, 0] for s in slots], axis=0)
        values = jnp.concatenate([kv_ref[s, 1] for s in slots], axis=0)
        sweep(j, keys, values, True)

    for j in range(nreq):

        @pl.when(active(j))
        def _():
            q_copy(j).wait()

    def request(j, carry):
        count = count_ref[number, base + j]
        groups = count // 8

        def eight(i, c):
            absorb(j, 8 * i, 8)
            return c

        lax.fori_loop(0, groups, eight, 0)
        for size in (4, 2, 1):

            @pl.when((count // size) % 2 == 1)
            def _():
                absorb(j, (count // (2 * size)) * (2 * size), size)

        return carry

    lax.fori_loop(0, nreq, request, 0)

    def finish(j, row, sums, values):
        for h in range(heads):
            done = values[row, h] * (1.0 / sums[row, pl.ds(h, 1), :])
            out_refs[j % 2][:, h * head_dim : (h + 1) * head_dim] = done.astype(jnp.bfloat16).T

    if last:
        for j in range(nreq):

            @pl.when(active(j))
            def _():
                finish(j, j, l_ref, acc_ref)

            @pl.when(jnp.logical_not(active(j)))
            def _():
                finish(j, base + j, state_in[1], state_in[2])


SHORT = pl.CostEstimate(flops=1, bytes_accessed=1, transcendentals=0)
SCOPED = 28 * 1024 * 1024
SMEM = pl.BlockSpec(memory_space=pltpu.SMEM)
VMEM = pl.BlockSpec(memory_space=pltpu.VMEM)
ANY = pl.BlockSpec(memory_space=pl.ANY)


def stage(number, work, queries, state, pieces, suffix=None, base=0, nreq=None, last=False):
    counts, lists = work
    half, heads, rows, head_dim = queries[0].shape
    own, _, block_tokens, _ = pieces[0].shape if pieces else (1, 2, 8, head_dim)
    first = suffix is not None
    nreq = nreq or 2 * half
    held = [
        pltpu.VMEM((nreq, heads, rows), jnp.float32),
        pltpu.VMEM((nreq, heads, rows), jnp.float32),
        pltpu.VMEM((nreq, heads, head_dim, rows), jnp.float32),
    ]
    scratch = (held if last else []) + [
        pltpu.VMEM((max(1, len(pieces)) * own, 2, block_tokens, head_dim), jnp.bfloat16),
        pltpu.VMEM((nreq, heads, rows, head_dim), jnp.bfloat16),
        pltpu.SemaphoreType.DMA((max(1, len(pieces)),)),
        pltpu.SemaphoreType.DMA((nreq,)),
    ]
    stats = jax.ShapeDtypeStruct((2 * half, heads, rows), jnp.float32)
    total = jax.ShapeDtypeStruct((2 * half, heads, head_dim, rows), jnp.float32)
    done = jax.ShapeDtypeStruct((rows, heads * head_dim), jnp.bfloat16)
    extra = suffix if first else state
    return pl.pallas_call(
        functools.partial(stage_kernel, len(pieces), own, number, first, last, base),
        in_specs=[SMEM, SMEM, ANY, ANY] + [VMEM] * len(extra) + [ANY] * len(pieces),
        out_specs=[VMEM] * 2 if last else [VMEM] * 3,
        out_shape=[done] * 2 if last else [stats, stats, total],
        scratch_shapes=scratch,
        compiler_params=pltpu.CompilerParams(vmem_limit_bytes=SCOPED),
        cost_estimate=SHORT,
        input_output_aliases={} if first or last else {4: 0, 5: 1, 6: 2},
    )(counts, lists, *queries, *extra, *pieces)


def project_kernel(start, core_ref, mine_ref, theirs_ref, weight_ref, out_ref):
    depth = mine_ref.shape[1]
    core = core_ref[0]
    columns = out_ref.shape[1]
    width = min(512, columns)
    for at in range(0, columns, width):
        across = pl.ds(start + at, width)
        summed = jnp.dot(
            mine_ref[...],
            weight_ref[pl.ds(core * depth, depth), across],
            preferred_element_type=jnp.float32,
        ) + jnp.dot(
            theirs_ref[...],
            weight_ref[pl.ds((1 - core) * depth, depth), across],
            preferred_element_type=jnp.float32,
        )
        out_ref[:, at : at + width] = summed.astype(out_ref.dtype)


def project(core, mine, theirs, out_weight, part, parts, dtype):
    columns = out_weight.shape[1] // parts
    return pl.pallas_call(
        functools.partial(project_kernel, part * columns),
        in_specs=[SMEM, VMEM, VMEM, VMEM],
        out_specs=VMEM,
        out_shape=jax.ShapeDtypeStruct((mine.shape[0], columns), dtype),
        compiler_params=pltpu.CompilerParams(vmem_limit_bytes=SCOPED),
        cost_estimate=SHORT,
    )(core.reshape(1), mine, theirs, out_weight)


def add_kernel(*refs):
    out_ref = refs[-1]
    count = (len(refs) - 1) // 2
    for i in range(count):
        kept, got = refs[i], refs[count + i]
        width = kept.shape[1]
        summed = kept[...].astype(jnp.float32) + got[...].astype(jnp.float32)
        out_ref[:, i * width : (i + 1) * width] = summed.astype(out_ref.dtype)


def add(kept, got):
    rows, width = kept[0].shape
    strip = rows // 4
    part = pl.BlockSpec((strip, width), lambda i: (i, 0))
    return pl.pallas_call(
        add_kernel,
        grid=(rows // strip,),
        in_specs=[part] * (2 * len(kept)),
        out_specs=pl.BlockSpec((strip, width * len(kept)), lambda i: (i, 0)),
        out_shape=jax.ShapeDtypeStruct((rows, width * len(kept)), jnp.bfloat16),
        compiler_params=pltpu.CompilerParams(vmem_limit_bytes=SCOPED),
        cost_estimate=SHORT,
    )(*kept, *got)


def ring_order(chips, at):
    half = chips // 2
    if chips == 8:
        place = jnp.where(at % 2 == 0, at // 2, chips - 1 - at // 2)
        chip = jnp.where(at < half, 2 * at, 2 * (chips - 1 - at) + 1)
    else:
        place = jnp.where(at < half, at, chips + half - 1 - at)
        chip = place
    return place, chip


def work_tables(plan, budgets, chips, own, group, lo, hi):
    most = max(len(pieces) for pieces in plan)
    filled = [pieces + [(0, -1)] * (most - len(pieces)) for pieces in plan]
    steps = jnp.asarray([[step for step, _ in pieces] for pieces in filled], jnp.int32)
    sides = jnp.asarray([[side for _, side in pieces] for pieces in filled], jnp.int32)
    place = ring_order(chips, group // CORES)[0]
    source = ring_order(chips, (place + steps + chips) % chips)[1]
    device = jnp.where(sides < 0, -chips * CORES, CORES * source + ((group % CORES) ^ sides))
    slots = jnp.arange(most * own)
    blocks = jnp.repeat(device * own, own, axis=1) + (slots % own)[None, :]
    inside = (blocks[:, None, None, :] >= lo[None, :, :, None]) & (
        blocks[:, None, None, :] < hi[None, :, :, None]
    )
    seen = jnp.any(inside, axis=2)
    number = jnp.sum(jnp.where(seen, 1, 0), axis=2)
    nreq = lo.shape[0]
    limit = jnp.asarray([budgets.get(i, 1 << 20) for i in range(len(plan))], jnp.int32)
    load, now = 0, []
    for j in range(nreq):
        fits = (load + number[:, j] <= limit) | (j < nreq // 2)
        load = load + jnp.where(fits, number[:, j], 0)
        now.append(fits)
    now = jnp.stack(now, axis=1)[:, :, None]
    left = jnp.concatenate(
        [(seen & ~now)[i] for i in sorted(budgets)] + [seen[-1, :, : len(plan[-1]) * own]], axis=1
    )
    size = left.shape[1]
    seen = jnp.pad(seen & now, ((0, 0), (0, 0), (0, size - most * own)))
    seen = jnp.concatenate([seen, left[None]], axis=0)
    slots = jnp.arange(size)
    ahead = slots[None, :] < slots[:, None]
    rank = jnp.sum(jnp.where(seen[:, :, None, :] & ahead, 1, 0), axis=3)
    here = seen[:, :, None, :] & (rank[:, :, None, :] == slots[:, None])
    lists = jnp.sum(jnp.where(here, slots, 0), axis=3)
    return jnp.sum(jnp.where(seen, 1, 0), axis=2).astype(jnp.int32), lists.astype(jnp.int32)


def on_device(chips, mems, queries, suffix_kv, prefix_kv, out_weight, node_blocks, root_of, mid_of):
    group = lax.axis_index("grp")
    mem = lax.axis_index("mem")
    core = group % CORES
    tokens_dev, heads_dev, head_dim = queries.shape
    reqs = tokens_dev // SUFFIX
    heads = heads_dev // CORES
    per_kv = QH // KVH
    own = prefix_kv.shape[0]
    half = chips // 2
    if chips == 8:
        ring = [0, 2, 4, 6, 7, 5, 3, 1]
    else:
        ring = list(range(half)) + list(range(half, chips))[::-1]

    swap = [(2 * s + c, 2 * s + 1 - c) for s in range(chips) for c in range(CORES)]
    ahead = [
        (2 * ring[i] + c, 2 * ring[(i + 1) % chips] + c) for i in range(chips) for c in range(CORES)
    ]
    behind = [(b, a) for a, b in ahead]

    kv_start = mem * heads_dev // per_kv
    kv_count = max(1, heads_dev // per_kv)

    def of_core(heads_kv, c):
        if kv_count == 1:
            return heads_kv[0]
        return jnp.where(c == 0, heads_kv[0], heads_kv[1])

    served = lax.dynamic_slice_in_dim(prefix_kv, kv_start, kv_count, 3)
    served = jnp.transpose(served, (3, 0, 1, 2, 4))
    own_a = of_core(served, core)
    own_b = lax.ppermute(of_core(served, 1 - core), "grp", swap)

    own_b, queries, suffix_kv, node_blocks, group = lax.optimization_barrier(
        (own_b, queries, suffix_kv, node_blocks, group)
    )

    order = (jnp.arange(reqs) + mem + 1) % reqs if mems == 2 else jnp.arange(reqs)

    def ordered(x):
        x = x.reshape((reqs, SUFFIX) + x.shape[1:])
        if mems != 2:
            return x
        return jnp.where(mem == 0, x[::-1], x)

    def query_part(c):
        return lax.dynamic_slice_in_dim(q_ordered, c * heads, heads, 1)

    q_ordered = jnp.transpose(ordered(queries), (0, 2, 1, 3))
    q = [query_part(core), lax.ppermute(query_part(1 - core), "grp", swap)]
    served = lax.dynamic_slice_in_dim(suffix_kv, kv_start, kv_count, 2)
    served = jnp.transpose(ordered(served), (3, 0, 2, 1, 4))
    suffix = [of_core(served, core), lax.ppermute(of_core(served, 1 - core), "grp", swap)]

    both = jnp.stack([group, group ^ 1])
    request_ids = (both[None, :] * reqs + order[:, None]).reshape(-1)
    lo, hi = path_ranges(request_ids, node_blocks, root_of, mid_of)
    far = chips // 2
    near = [[(-k, 0), (-k, 1), (k, 0), (k, 1)] for k in range(1, far)]
    final_plan = [(-far, 0), (far, 1)]
    plan = [[(0, 0), (0, 1)]] + near + [final_plan]
    budgets = {far - 2: 24, far - 1: 16}
    work = work_tables(plan, budgets, chips, own, group, lo, hi)

    def tied(x, y, state):
        return lax.optimization_barrier((x, y, state))

    state = stage(0, work, q, None, [], suffix=suffix)
    forth, back = [own_a, own_b], [own_a, own_b]
    for k in range(1, far):
        forth = [lax.ppermute(x, "grp", ahead) for x in forth]
        back = [lax.ppermute(x, "grp", behind) for x in back]
        if k == 1:
            forth[0], back[0], state = tied(forth[0], back[0], state)
            state = stage(0, work, q, state, [own_a, own_b])
        else:
            forth[0], back[0], state = tied(forth[0], back[0], state)
            state = stage(k - 1, work, q, state, last_step)
            before_last = last_step
        forth[1], back[1], state = tied(forth[1], back[1], state)
        last_step = forth + back
    step = forth + back
    state = stage(far - 1, work, q, state, step)
    final = [lax.ppermute(forth[0], "grp", ahead), lax.ppermute(back[1], "grp", behind)]

    def attended(part, state):
        number, pieces = (far, final) if part == 0 else (far + 1, before_last + step + final)
        staying, leaving = stage(
            number, work, q, state, pieces, base=2 * part, nreq=2, last=True
        )
        return staying, lax.ppermute(leaving, "grp", swap)

    if mems != 2:
        rows = [
            project(core, *attended(k, state), out_weight, 0, 1, jnp.bfloat16) for k in range(reqs)
        ]
        return lax.psum_scatter(
            jnp.concatenate(rows, axis=0), "mem", scatter_dimension=0, tiled=True
        )

    def exchange(x):
        return lax.ppermute(x, "mem", [(0, 1), (1, 0)])

    def part_of(rows, i, dtype):
        return project(core, *rows, out_weight, i, 2, dtype)

    def follows(work_now, *now):
        shapes = jax.eval_shape(work_now, *now)
        return lax.cond(
            node_blocks[0] >= 0,
            work_now,
            lambda *_: jax.tree.map(lambda x: jnp.zeros(x.shape, x.dtype), shapes),
            *now,
        )

    def keep(state):
        rows = attended(1, state)
        return [part_of(rows, i, jnp.bfloat16) for i in range(2)]

    def second(rows, state):
        sent, state = lax.optimization_barrier((part_of(rows, 1, jnp.bfloat16), state))
        got = exchange(sent)
        kept = follows(keep, state)
        return got, kept

    rows = attended(0, state)
    sent, rows, state = lax.optimization_barrier((part_of(rows, 0, jnp.bfloat16), rows, state))
    got = [exchange(sent)]
    late, kept = follows(second, rows, state)
    got.append(late)
    return add(kept, got)


def solution(mesh):
    return jax.shard_map(
        functools.partial(on_device, mesh.shape["grp"] // CORES, mesh.shape["mem"]),
        mesh=mesh,
        in_specs=(
            P("grp", "mem", None),
            P("grp", None, None, None),
            P("grp", None, None, None, None),
            P("mem", None),
            P(),
            P(),
            P(),
        ),
        out_specs=P(("grp", "mem"), None),
        check_vma=False,
    )
```

```python
import functools

import jax
import jax.numpy as jnp
from jax import lax
from jax.experimental import pallas as pl
from jax.experimental.pallas import tpu as pltpu
from jax.sharding import PartitionSpec as P

QH = 32
KVH = 4
SUFFIX = 256
CORES = 2
NEG = -1e30


def path_ranges(request_ids, node_blocks, root_of, mid_of):
    nodes_all = node_blocks.shape[0]
    middles_all = root_of.shape[0]
    leaves = mid_of.shape[0]
    roots_all = nodes_all - middles_all - leaves
    firsts = jnp.cumsum(node_blocks) - node_blocks
    middles = jnp.sum(
        jnp.where(jnp.arange(leaves)[None, :] == request_ids[:, None], mid_of[None, :], 0), axis=1
    )
    root_ids = jnp.sum(
        jnp.where(jnp.arange(middles_all)[None, :] == middles[:, None], root_of[None, :], 0), axis=1
    )
    path_nodes = jnp.stack(
        [root_ids, roots_all + middles, roots_all + middles_all + request_ids], axis=1
    )
    picked = jnp.arange(nodes_all)[None, None, :] == path_nodes[:, :, None]
    lower_end = jnp.sum(jnp.where(picked, firsts[None, None, :], 0), axis=2)
    upper_end = lower_end + jnp.sum(jnp.where(picked, node_blocks[None, None, :], 0), axis=2)
    return (lower_end, upper_end)


def stage_kernel(n_pieces, own, number, first, last, base, *refs):
    refs = list(refs)
    count_ref, list_ref, mine_ref, theirs_ref = refs[:4]
    refs = refs[4:]
    if first:
        suffix_refs, refs = refs[:2], refs[2:]
    else:
        state_in, refs = refs[:3], refs[3:]
    pieces, refs = refs[:n_pieces], refs[n_pieces:]
    if last:
        out_refs, state_refs, refs = refs[:2], refs[2:5], refs[5:]
        m_ref, l_ref, acc_ref = state_refs
    else:
        m_ref, l_ref, acc_ref = refs[:3]
        refs = refs[3:]
    kv_ref, q_ref, piece_sems, q_sems = refs
    nreq, heads, rows, head_dim = q_ref.shape
    scale = head_dim ** (-0.5)
    first_row = 0 if last else base

    def q_copy(j):
        source = (mine_ref, theirs_ref)[(base + j) % 2].at[(base + j) // 2]
        return pltpu.make_async_copy(source, q_ref.at[j], q_sems.at[j])

    def piece_copy(i):
        return pltpu.make_async_copy(
            pieces[i], kv_ref.at[pl.ds(i * own, own)], piece_sems.at[i]
        )

    def active(j):
        return count_ref[number, base + j] > 0

    if first:
        for j in range(nreq):
            q_copy(j).start()
    else:
        work = active(0)
        for j in range(1, nreq):
            work = work | active(j)

        @pl.when(work)
        def _():
            for i in range(n_pieces):
                piece_copy(i).start()

        for j in range(nreq):

            @pl.when(active(j))
            def _():
                q_copy(j).start()
                if last:
                    for mine, given in zip(state_refs, state_in):
                        mine[j] = given[base + j]

    def dot(a, b):
        return jnp.dot(a, b, preferred_element_type=jnp.float32)

    def sweep(j, keys, values, old, mask=None):
        size = values.shape[0]
        values = jnp.concatenate([values.T, jnp.ones((16, size), jnp.bfloat16)], axis=0)
        scores, weights, tops, totals = {}, {}, [], []
        if old:
            highest, sums = m_ref[first_row + j], l_ref[first_row + j]
        for t in range(heads + 3):
            if t < heads:
                scores[t] = lax.dot_general(
                    keys, q_ref[j, t], (((1,), (1,)), ((), ())), preferred_element_type=jnp.float32
                )
            h = t - 3
            if h >= 0:
                p, factor = weights.pop(h)
                summed = dot(values, p)
                total = summed[head_dim : head_dim + 1]
                if old:
                    acc_ref[first_row + j, h] = acc_ref[first_row + j, h] * factor + summed[:head_dim]
                    total = sums[h : h + 1] * factor + total
                else:
                    acc_ref[first_row + j, h] = summed[:head_dim]
                totals.append(total)
            h = t - 2
            if 0 <= h < heads:
                s = scores.pop(h)
                if mask is not None:
                    s = jnp.where(mask, s, NEG)
                top = jnp.max(s, axis=0, keepdims=True)
                factor = None
                if old:
                    before = highest[h : h + 1]
                    top = jnp.maximum(before, top)
                    factor = jnp.exp((before - top) * scale)
                tops.append(top)
                p = jnp.exp((s - top).astype(jnp.bfloat16) * jnp.bfloat16(scale))
                weights[h] = (p, factor)
        m_ref[first_row + j] = jnp.concatenate(tops, axis=0)
        l_ref[first_row + j] = jnp.concatenate(totals, axis=0)

    if first:
        key_at = lax.broadcasted_iota(jnp.int32, (rows, rows), 0)
        row_at = lax.broadcasted_iota(jnp.int32, (rows, rows), 1)
        for j in range(nreq):
            q_copy(j).wait()
        for side in range(2):

            def start(k, carry, side=side):
                sfx = suffix_refs[side]
                sweep(2 * k + side, sfx[k, 0], sfx[k, 1], False, key_at <= row_at)
                return carry

            lax.fori_loop(0, nreq // 2, start, 0)

        return

    @pl.when(work)
    def _():
        for i in range(n_pieces):
            piece_copy(i).wait()

    def absorb(j, at, count):
        slots = [list_ref[number, base + j, at + u] for u in range(count)]
        keys = jnp.concatenate([kv_ref[s, 0] for s in slots], axis=0)
        values = jnp.concatenate([kv_ref[s, 1] for s in slots], axis=0)
        sweep(j, keys, values, True)

    for j in range(nreq):

        @pl.when(active(j))
        def _():
            q_copy(j).wait()

    def request(j, carry):
        count = count_ref[number, base + j]
        groups = count // 8

        def eight(i, c):
            absorb(j, 8 * i, 8)
            return c

        lax.fori_loop(0, groups, eight, 0)
        for size in (4, 2, 1):

            @pl.when((count // size) % 2 == 1)
            def _():
                absorb(j, (count // (2 * size)) * (2 * size), size)

        return carry

    lax.fori_loop(0, nreq, request, 0)

    def finish(j, row, sums, values):
        for h in range(heads):
            done = values[row, h] * (1.0 / sums[row, pl.ds(h, 1), :])
            out_refs[j % 2][:, h * head_dim : (h + 1) * head_dim] = done.astype(jnp.bfloat16).T

    if last:
        for j in range(nreq):

            @pl.when(active(j))
            def _():
                finish(j, j, l_ref, acc_ref)

            @pl.when(jnp.logical_not(active(j)))
            def _():
                finish(j, base + j, state_in[1], state_in[2])


SHORT = pl.CostEstimate(flops=1, bytes_accessed=1, transcendentals=0)
SCOPED = 28 * 1024 * 1024
SMEM = pl.BlockSpec(memory_space=pltpu.SMEM)
VMEM = pl.BlockSpec(memory_space=pltpu.VMEM)
ANY = pl.BlockSpec(memory_space=pl.ANY)


def stage(number, work, queries, state, pieces, suffix=None, base=0, nreq=None, last=False):
    counts, lists = work
    half, heads, rows, head_dim = queries[0].shape
    own, _, block_tokens, _ = pieces[0].shape if pieces else (1, 2, 8, head_dim)
    first = suffix is not None
    nreq = nreq or 2 * half
    held = [
        pltpu.VMEM((nreq, heads, rows), jnp.float32),
        pltpu.VMEM((nreq, heads, rows), jnp.float32),
        pltpu.VMEM((nreq, heads, head_dim, rows), jnp.float32),
    ]
    scratch = (held if last else []) + [
        pltpu.VMEM((max(1, len(pieces)) * own, 2, block_tokens, head_dim), jnp.bfloat16),
        pltpu.VMEM((nreq, heads, rows, head_dim), jnp.bfloat16),
        pltpu.SemaphoreType.DMA((max(1, len(pieces)),)),
        pltpu.SemaphoreType.DMA((nreq,)),
    ]
    stats = jax.ShapeDtypeStruct((2 * half, heads, rows), jnp.float32)
    total = jax.ShapeDtypeStruct((2 * half, heads, head_dim, rows), jnp.float32)
    done = jax.ShapeDtypeStruct((rows, heads * head_dim), jnp.bfloat16)
    extra = suffix if first else state
    return pl.pallas_call(
        functools.partial(stage_kernel, len(pieces), own, number, first, last, base),
        in_specs=[SMEM, SMEM, ANY, ANY] + [VMEM] * len(extra) + [ANY] * len(pieces),
        out_specs=[VMEM] * 2 if last else [VMEM] * 3,
        out_shape=[done] * 2 if last else [stats, stats, total],
        scratch_shapes=scratch,
        compiler_params=pltpu.CompilerParams(vmem_limit_bytes=SCOPED),
        cost_estimate=SHORT,
        input_output_aliases={} if first or last else {4: 0, 5: 1, 6: 2},
    )(counts, lists, *queries, *extra, *pieces)


def project_kernel(start, core_ref, mine_ref, theirs_ref, weight_ref, out_ref):
    depth = mine_ref.shape[1]
    core = core_ref[0]
    columns = out_ref.shape[1]
    width = min(512, columns)
    for at in range(0, columns, width):
        across = pl.ds(start + at, width)
        summed = jnp.dot(
            mine_ref[...],
            weight_ref[pl.ds(core * depth, depth), across],
            preferred_element_type=jnp.float32,
        ) + jnp.dot(
            theirs_ref[...],
            weight_ref[pl.ds((1 - core) * depth, depth), across],
            preferred_element_type=jnp.float32,
        )
        out_ref[:, at : at + width] = summed.astype(out_ref.dtype)


def project(core, mine, theirs, out_weight, part, parts, dtype):
    columns = out_weight.shape[1] // parts
    return pl.pallas_call(
        functools.partial(project_kernel, part * columns),
        in_specs=[SMEM, VMEM, VMEM, VMEM],
        out_specs=VMEM,
        out_shape=jax.ShapeDtypeStruct((mine.shape[0], columns), dtype),
        compiler_params=pltpu.CompilerParams(vmem_limit_bytes=SCOPED),
        cost_estimate=SHORT,
    )(core.reshape(1), mine, theirs, out_weight)


def add_kernel(*refs):
    out_ref = refs[-1]
    count = (len(refs) - 1) // 2
    for i in range(count):
        kept, got = refs[i], refs[count + i]
        width = kept.shape[1]
        summed = kept[...].astype(jnp.float32) + got[...].astype(jnp.float32)
        out_ref[:, i * width : (i + 1) * width] = summed.astype(out_ref.dtype)


def add(kept, got):
    rows, width = kept[0].shape
    return pl.pallas_call(
        add_kernel,
        in_specs=[VMEM] * (2 * len(kept)),
        out_specs=VMEM,
        out_shape=jax.ShapeDtypeStruct((rows, width * len(kept)), jnp.bfloat16),
        compiler_params=pltpu.CompilerParams(vmem_limit_bytes=SCOPED),
        cost_estimate=SHORT,
    )(*kept, *got)


def ring_order(chips, at):
    half = chips // 2
    if chips == 8:
        place = jnp.where(at % 2 == 0, at // 2, chips - 1 - at // 2)
        chip = jnp.where(at < half, 2 * at, 2 * (chips - 1 - at) + 1)
    else:
        place = jnp.where(at < half, at, chips + half - 1 - at)
        chip = place
    return place, chip


def work_tables(plan, budgets, chips, own, group, lo, hi):
    most = max(len(pieces) for pieces in plan)
    filled = [pieces + [(0, -1)] * (most - len(pieces)) for pieces in plan]
    steps = jnp.asarray([[step for step, _ in pieces] for pieces in filled], jnp.int32)
    sides = jnp.asarray([[side for _, side in pieces] for pieces in filled], jnp.int32)
    place = ring_order(chips, group // CORES)[0]
    source = ring_order(chips, (place + steps + chips) % chips)[1]
    device = jnp.where(sides < 0, -chips * CORES, CORES * source + ((group % CORES) ^ sides))
    slots = jnp.arange(most * own)
    blocks = jnp.repeat(device * own, own, axis=1) + (slots % own)[None, :]
    inside = (blocks[:, None, None, :] >= lo[None, :, :, None]) & (
        blocks[:, None, None, :] < hi[None, :, :, None]
    )
    seen = jnp.any(inside, axis=2)
    number = jnp.sum(jnp.where(seen, 1, 0), axis=2)
    nreq = lo.shape[0]
    limit = jnp.asarray([budgets.get(i, 1 << 20) for i in range(len(plan))], jnp.int32)
    load, taken = 0, []
    for j in range(nreq):
        room = number[:, j] if j < nreq // 2 else jnp.clip(limit - load, 0, number[:, j])
        load = load + room
        taken.append(room)
    before = slots[None, :] < slots[:, None]
    rank = jnp.sum(jnp.where(seen[:, :, None, :] & before, 1, 0), axis=3)
    now = rank < jnp.stack(taken, axis=1)[:, :, None]
    left = jnp.concatenate(
        [(seen & ~now)[i] for i in sorted(budgets)] + [seen[-1, :, : len(plan[-1]) * own]], axis=1
    )
    size = left.shape[1]
    seen = jnp.pad(seen & now, ((0, 0), (0, 0), (0, size - most * own)))
    seen = jnp.concatenate([seen, left[None]], axis=0)
    slots = jnp.arange(size)
    ahead = slots[None, :] < slots[:, None]
    rank = jnp.sum(jnp.where(seen[:, :, None, :] & ahead, 1, 0), axis=3)
    here = seen[:, :, None, :] & (rank[:, :, None, :] == slots[:, None])
    lists = jnp.sum(jnp.where(here, slots, 0), axis=3)
    return jnp.sum(jnp.where(seen, 1, 0), axis=2).astype(jnp.int32), lists.astype(jnp.int32)


def on_device(chips, mems, queries, suffix_kv, prefix_kv, out_weight, node_blocks, root_of, mid_of):
    group = lax.axis_index("grp")
    mem = lax.axis_index("mem")
    core = group % CORES
    tokens_dev, heads_dev, head_dim = queries.shape
    reqs = tokens_dev // SUFFIX
    heads = heads_dev // CORES
    per_kv = QH // KVH
    own = prefix_kv.shape[0]
    half = chips // 2
    if chips == 8:
        ring = [0, 2, 4, 6, 7, 5, 3, 1]
    else:
        ring = list(range(half)) + list(range(half, chips))[::-1]

    swap = [(2 * s + c, 2 * s + 1 - c) for s in range(chips) for c in range(CORES)]
    ahead = [
        (2 * ring[i] + c, 2 * ring[(i + 1) % chips] + c) for i in range(chips) for c in range(CORES)
    ]
    behind = [(b, a) for a, b in ahead]

    kv_start = mem * heads_dev // per_kv
    kv_count = max(1, heads_dev // per_kv)

    def of_core(heads_kv, c):
        if kv_count == 1:
            return heads_kv[0]
        return jnp.where(c == 0, heads_kv[0], heads_kv[1])

    served = lax.dynamic_slice_in_dim(prefix_kv, kv_start, kv_count, 3)
    served = jnp.transpose(served, (3, 0, 1, 2, 4))
    own_a = of_core(served, core)
    own_b = lax.ppermute(of_core(served, 1 - core), "grp", swap)

    own_b, queries, suffix_kv, node_blocks, group = lax.optimization_barrier(
        (own_b, queries, suffix_kv, node_blocks, group)
    )

    order = (jnp.arange(reqs) + mem + 1) % reqs if mems == 2 else jnp.arange(reqs)

    def ordered(x):
        x = x.reshape((reqs, SUFFIX) + x.shape[1:])
        if mems != 2:
            return x
        return jnp.where(mem == 0, x[::-1], x)

    def query_part(c):
        return lax.dynamic_slice_in_dim(q_ordered, c * heads, heads, 1)

    q_ordered = jnp.transpose(ordered(queries), (0, 2, 1, 3))
    q = [query_part(core), lax.ppermute(query_part(1 - core), "grp", swap)]
    served = lax.dynamic_slice_in_dim(suffix_kv, kv_start, kv_count, 2)
    served = jnp.transpose(ordered(served), (3, 0, 2, 1, 4))
    suffix = [of_core(served, core), lax.ppermute(of_core(served, 1 - core), "grp", swap)]

    both = jnp.stack([group, group ^ 1])
    request_ids = (both[None, :] * reqs + order[:, None]).reshape(-1)
    lo, hi = path_ranges(request_ids, node_blocks, root_of, mid_of)
    far = chips // 2
    near = [[(-k, 0), (-k, 1), (k, 0), (k, 1)] for k in range(1, far)]
    final_plan = [(-far, 0), (far, 1)]
    plan = [[(0, 0), (0, 1)]] + near + [final_plan]
    budgets = {far - 2: 30, far - 1: 22}
    work = work_tables(plan, budgets, chips, own, group, lo, hi)

    def tied(x, y, state):
        return lax.optimization_barrier((x, y, state))

    state = stage(0, work, q, None, [], suffix=suffix)
    forth, back = [own_a, own_b], [own_a, own_b]
    for k in range(1, far):
        forth = [lax.ppermute(x, "grp", ahead) for x in forth]
        back = [lax.ppermute(x, "grp", behind) for x in back]
        if k == 1:
            forth[0], back[0], state = tied(forth[0], back[0], state)
            state = stage(0, work, q, state, [own_a, own_b])
        else:
            forth[0], back[0], state = tied(forth[0], back[0], state)
            state = stage(k - 1, work, q, state, last_step)
            before_last = last_step
        forth[1], back[1], state = tied(forth[1], back[1], state)
        last_step = forth + back
    step = forth + back
    state = stage(far - 1, work, q, state, step)
    final = [lax.ppermute(forth[0], "grp", ahead), lax.ppermute(back[1], "grp", behind)]

    def attended(part, state):
        number, pieces = (far, final) if part == 0 else (far + 1, before_last + step + final)
        staying, leaving = stage(
            number, work, q, state, pieces, base=2 * part, nreq=2, last=True
        )
        return staying, lax.ppermute(leaving, "grp", swap)

    if mems != 2:
        rows = [
            project(core, *attended(k, state), out_weight, 0, 1, jnp.bfloat16) for k in range(reqs)
        ]
        return lax.psum_scatter(
            jnp.concatenate(rows, axis=0), "mem", scatter_dimension=0, tiled=True
        )

    def exchange(x):
        return lax.ppermute(x, "mem", [(0, 1), (1, 0)])

    def part_of(rows, i, dtype):
        return project(core, *rows, out_weight, i, 2, dtype)

    def follows(work_now, *now):
        shapes = jax.eval_shape(work_now, *now)
        return lax.cond(
            node_blocks[0] >= 0,
            work_now,
            lambda *_: jax.tree.map(lambda x: jnp.zeros(x.shape, x.dtype), shapes),
            *now,
        )

    def keep(state):
        rows = attended(1, state)
        return [part_of(rows, i, jnp.bfloat16) for i in range(2)]

    def second(rows, state):
        sent, state = lax.optimization_barrier((part_of(rows, 1, jnp.bfloat16), state))
        got = exchange(sent)
        kept = follows(keep, state)
        return got, kept

    rows = attended(0, state)
    sent, rows, state = lax.optimization_barrier((part_of(rows, 0, jnp.bfloat16), rows, state))
    got = [exchange(sent)]
    late, kept = follows(second, rows, state)
    got.append(late)
    return add(kept, got)


def solution(mesh):
    return jax.shard_map(
        functools.partial(on_device, mesh.shape["grp"] // CORES, mesh.shape["mem"]),
        mesh=mesh,
        in_specs=(
            P("grp", "mem", None),
            P("grp", None, None, None),
            P("grp", None, None, None, None),
            P("mem", None),
            P(),
            P(),
            P(),
        ),
        out_specs=P(("grp", "mem"), None),
        check_vma=False,
    )
```

```python
import functools

import jax
import jax.numpy as jnp
from jax import lax
from jax.experimental import pallas as pl
from jax.experimental.pallas import tpu as pltpu
from jax.sharding import PartitionSpec as P

QH = 32
KVH = 4
SUFFIX = 256
CORES = 2
NEG = -1e30


def path_ranges(request_ids, node_blocks, root_of, mid_of):
    nodes_all = node_blocks.shape[0]
    middles_all = root_of.shape[0]
    leaves = mid_of.shape[0]
    roots_all = nodes_all - middles_all - leaves
    firsts = jnp.cumsum(node_blocks) - node_blocks
    middles = jnp.sum(
        jnp.where(jnp.arange(leaves)[None, :] == request_ids[:, None], mid_of[None, :], 0), axis=1
    )
    root_ids = jnp.sum(
        jnp.where(jnp.arange(middles_all)[None, :] == middles[:, None], root_of[None, :], 0), axis=1
    )
    path_nodes = jnp.stack(
        [root_ids, roots_all + middles, roots_all + middles_all + request_ids], axis=1
    )
    picked = jnp.arange(nodes_all)[None, None, :] == path_nodes[:, :, None]
    lower_end = jnp.sum(jnp.where(picked, firsts[None, None, :], 0), axis=2)
    upper_end = lower_end + jnp.sum(jnp.where(picked, node_blocks[None, None, :], 0), axis=2)
    return (lower_end, upper_end)


def stage_kernel(n_pieces, own, number, first, last, base, *refs):
    refs = list(refs)
    count_ref, list_ref, mine_ref, theirs_ref = refs[:4]
    refs = refs[4:]
    if first:
        suffix_refs, refs = refs[:2], refs[2:]
    else:
        state_in, refs = refs[:3], refs[3:]
    pieces, refs = refs[:n_pieces], refs[n_pieces:]
    if last:
        out_refs, state_refs, refs = refs[:2], refs[2:5], refs[5:]
        m_ref, l_ref, acc_ref = state_refs
    else:
        m_ref, l_ref, acc_ref = refs[:3]
        refs = refs[3:]
    kv_ref, q_ref, piece_sems, q_sems = refs
    nreq, heads, rows, head_dim = q_ref.shape
    scale = head_dim ** (-0.5)
    first_row = 0 if last else base

    def q_copy(j):
        source = (mine_ref, theirs_ref)[(base + j) % 2].at[(base + j) // 2]
        return pltpu.make_async_copy(source, q_ref.at[j], q_sems.at[j])

    def piece_copy(i):
        return pltpu.make_async_copy(
            pieces[i], kv_ref.at[pl.ds(i * own, own)], piece_sems.at[i]
        )

    def active(j):
        return count_ref[number, base + j] > 0

    if first:
        for j in range(nreq):
            q_copy(j).start()
    else:
        work = active(0)
        for j in range(1, nreq):
            work = work | active(j)

        @pl.when(work)
        def _():
            for i in range(n_pieces):
                piece_copy(i).start()

        for j in range(nreq):

            @pl.when(active(j))
            def _():
                q_copy(j).start()
                if last:
                    for mine, given in zip(state_refs, state_in):
                        mine[j] = given[base + j]

    def dot(a, b):
        return jnp.dot(a, b, preferred_element_type=jnp.float32)

    def sweep(j, keys, values, old, mask=None):
        size = values.shape[0]
        values = jnp.concatenate([values.T, jnp.ones((16, size), jnp.bfloat16)], axis=0)
        scores, weights, tops, totals = {}, {}, [], []
        if old:
            highest, sums = m_ref[first_row + j], l_ref[first_row + j]
        for t in range(heads + 3):
            if t < heads:
                scores[t] = lax.dot_general(
                    keys, q_ref[j, t], (((1,), (1,)), ((), ())), preferred_element_type=jnp.float32
                )
            h = t - 3
            if h >= 0:
                p, factor = weights.pop(h)
                summed = dot(values, p)
                total = summed[head_dim : head_dim + 1]
                if old:
                    acc_ref[first_row + j, h] = acc_ref[first_row + j, h] * factor + summed[:head_dim]
                    total = sums[h : h + 1] * factor + total
                else:
                    acc_ref[first_row + j, h] = summed[:head_dim]
                totals.append(total)
            h = t - 2
            if 0 <= h < heads:
                s = scores.pop(h)
                if mask is not None:
                    s = jnp.where(mask, s, NEG)
                top = jnp.max(s, axis=0, keepdims=True)
                factor = None
                if old:
                    before = highest[h : h + 1]
                    top = jnp.maximum(before, top)
                    factor = jnp.exp((before - top) * scale)
                tops.append(top)
                p = jnp.exp((s - top).astype(jnp.bfloat16) * jnp.bfloat16(scale))
                weights[h] = (p, factor)
        m_ref[first_row + j] = jnp.concatenate(tops, axis=0)
        l_ref[first_row + j] = jnp.concatenate(totals, axis=0)

    if first:
        key_at = lax.broadcasted_iota(jnp.int32, (rows, rows), 0)
        row_at = lax.broadcasted_iota(jnp.int32, (rows, rows), 1)
        for j in range(nreq):
            q_copy(j).wait()
        for side in range(2):

            def start(k, carry, side=side):
                sfx = suffix_refs[side]
                sweep(2 * k + side, sfx[k, 0], sfx[k, 1], False, key_at <= row_at)
                return carry

            lax.fori_loop(0, nreq // 2, start, 0)

        return

    @pl.when(work)
    def _():
        for i in range(n_pieces):
            piece_copy(i).wait()

    def absorb(j, at, count):
        slots = [list_ref[number, base + j, at + u] for u in range(count)]
        keys = jnp.concatenate([kv_ref[s, 0] for s in slots], axis=0)
        values = jnp.concatenate([kv_ref[s, 1] for s in slots], axis=0)
        sweep(j, keys, values, True)

    for j in range(nreq):

        @pl.when(active(j))
        def _():
            q_copy(j).wait()

    def request(j, carry):
        count = count_ref[number, base + j]
        groups = count // 8

        def eight(i, c):
            absorb(j, 8 * i, 8)
            return c

        lax.fori_loop(0, groups, eight, 0)
        for size in (4, 2, 1):

            @pl.when((count // size) % 2 == 1)
            def _():
                absorb(j, (count // (2 * size)) * (2 * size), size)

        return carry

    lax.fori_loop(0, nreq, request, 0)

    def finish(j, row, sums, values):
        for h in range(heads):
            done = values[row, h] * (1.0 / sums[row, pl.ds(h, 1), :])
            out_refs[j % 2][:, h * head_dim : (h + 1) * head_dim] = done.astype(jnp.bfloat16).T

    if last:
        for j in range(nreq):

            @pl.when(active(j))
            def _():
                finish(j, j, l_ref, acc_ref)

            @pl.when(jnp.logical_not(active(j)))
            def _():
                finish(j, base + j, state_in[1], state_in[2])


SHORT = pl.CostEstimate(flops=1, bytes_accessed=1, transcendentals=0)
SCOPED = 28 * 1024 * 1024
SMEM = pl.BlockSpec(memory_space=pltpu.SMEM)
VMEM = pl.BlockSpec(memory_space=pltpu.VMEM)
ANY = pl.BlockSpec(memory_space=pl.ANY)


def stage(number, work, queries, state, pieces, suffix=None, base=0, nreq=None, last=False):
    counts, lists = work
    half, heads, rows, head_dim = queries[0].shape
    own, _, block_tokens, _ = pieces[0].shape if pieces else (1, 2, 8, head_dim)
    first = suffix is not None
    nreq = nreq or 2 * half
    held = [
        pltpu.VMEM((nreq, heads, rows), jnp.float32),
        pltpu.VMEM((nreq, heads, rows), jnp.float32),
        pltpu.VMEM((nreq, heads, head_dim, rows), jnp.float32),
    ]
    scratch = (held if last else []) + [
        pltpu.VMEM((max(1, len(pieces)) * own, 2, block_tokens, head_dim), jnp.bfloat16),
        pltpu.VMEM((nreq, heads, rows, head_dim), jnp.bfloat16),
        pltpu.SemaphoreType.DMA((max(1, len(pieces)),)),
        pltpu.SemaphoreType.DMA((nreq,)),
    ]
    stats = jax.ShapeDtypeStruct((2 * half, heads, rows), jnp.float32)
    total = jax.ShapeDtypeStruct((2 * half, heads, head_dim, rows), jnp.float32)
    done = jax.ShapeDtypeStruct((rows, heads * head_dim), jnp.bfloat16)
    extra = suffix if first else state
    return pl.pallas_call(
        functools.partial(stage_kernel, len(pieces), own, number, first, last, base),
        in_specs=[SMEM, SMEM, ANY, ANY] + [VMEM] * len(extra) + [ANY] * len(pieces),
        out_specs=[VMEM] * 2 if last else [VMEM] * 3,
        out_shape=[done] * 2 if last else [stats, stats, total],
        scratch_shapes=scratch,
        compiler_params=pltpu.CompilerParams(vmem_limit_bytes=SCOPED),
        cost_estimate=SHORT,
        input_output_aliases={} if first or last else {4: 0, 5: 1, 6: 2},
    )(counts, lists, *queries, *extra, *pieces)


def project_kernel(start, core_ref, mine_ref, theirs_ref, weight_ref, out_ref):
    depth = mine_ref.shape[1]
    core = core_ref[0]
    columns = out_ref.shape[1]
    width = min(512, columns)
    for at in range(0, columns, width):
        across = pl.ds(start + at, width)
        summed = jnp.dot(
            mine_ref[...],
            weight_ref[pl.ds(core * depth, depth), across],
            preferred_element_type=jnp.float32,
        ) + jnp.dot(
            theirs_ref[...],
            weight_ref[pl.ds((1 - core) * depth, depth), across],
            preferred_element_type=jnp.float32,
        )
        out_ref[:, at : at + width] = summed.astype(out_ref.dtype)


def project(core, mine, theirs, out_weight, start=0, columns=None):
    columns = columns or out_weight.shape[1]
    return pl.pallas_call(
        functools.partial(project_kernel, start),
        in_specs=[SMEM, VMEM, VMEM, VMEM],
        out_specs=VMEM,
        out_shape=jax.ShapeDtypeStruct((mine.shape[0], columns), jnp.bfloat16),
        compiler_params=pltpu.CompilerParams(vmem_limit_bytes=SCOPED),
        cost_estimate=SHORT,
    )(core.reshape(1), mine, theirs, out_weight)


def add_kernel(kept_ref, *refs):
    *got_refs, out_ref = refs
    at = 0
    for got in got_refs:
        part = slice(at, at + got.shape[1])
        summed = kept_ref[:, part].astype(jnp.float32) + got[...].astype(jnp.float32)
        out_ref[:, part] = summed.astype(out_ref.dtype)
        at += got.shape[1]


def add(kept, *got):
    return pl.pallas_call(
        add_kernel,
        in_specs=[VMEM] * (1 + len(got)),
        out_specs=VMEM,
        out_shape=jax.ShapeDtypeStruct(kept.shape, jnp.bfloat16),
        compiler_params=pltpu.CompilerParams(vmem_limit_bytes=SCOPED),
        cost_estimate=SHORT,
    )(kept, *got)


def ring_order(chips, at):
    half = chips // 2
    if chips == 8:
        place = jnp.where(at % 2 == 0, at // 2, chips - 1 - at // 2)
        chip = jnp.where(at < half, 2 * at, 2 * (chips - 1 - at) + 1)
    else:
        place = jnp.where(at < half, at, chips + half - 1 - at)
        chip = place
    return place, chip


def work_tables(plan, budgets, chips, own, group, lo, hi):
    most = max(len(pieces) for pieces in plan)
    filled = [pieces + [(0, -1)] * (most - len(pieces)) for pieces in plan]
    steps = jnp.asarray([[step for step, _ in pieces] for pieces in filled], jnp.int32)
    sides = jnp.asarray([[side for _, side in pieces] for pieces in filled], jnp.int32)
    place = ring_order(chips, group // CORES)[0]
    source = ring_order(chips, (place + steps + chips) % chips)[1]
    device = jnp.where(sides < 0, -chips * CORES, CORES * source + ((group % CORES) ^ sides))
    slots = jnp.arange(most * own)
    blocks = jnp.repeat(device * own, own, axis=1) + (slots % own)[None, :]
    inside = (blocks[:, None, None, :] >= lo[None, :, :, None]) & (
        blocks[:, None, None, :] < hi[None, :, :, None]
    )
    seen = jnp.any(inside, axis=2)
    number = jnp.sum(jnp.where(seen, 1, 0), axis=2)
    nreq = lo.shape[0]
    limit = jnp.asarray([budgets.get(i, 1 << 20) for i in range(len(plan))], jnp.int32)
    load, taken = 0, []
    for j in range(nreq):
        room = number[:, j] if j < nreq // 2 else jnp.clip(limit - load, 0, number[:, j])
        load = load + room
        taken.append(room)
    before = slots[None, :] < slots[:, None]
    rank = jnp.sum(jnp.where(seen[:, :, None, :] & before, 1, 0), axis=3)
    now = rank < jnp.stack(taken, axis=1)[:, :, None]
    left = jnp.concatenate(
        [(seen & ~now)[i] for i in sorted(budgets)] + [seen[-1, :, : len(plan[-1]) * own]], axis=1
    )
    size = left.shape[1]
    seen = jnp.pad(seen & now, ((0, 0), (0, 0), (0, size - most * own)))
    seen = jnp.concatenate([seen, left[None]], axis=0)
    slots = jnp.arange(size)
    ahead = slots[None, :] < slots[:, None]
    rank = jnp.sum(jnp.where(seen[:, :, None, :] & ahead, 1, 0), axis=3)
    here = seen[:, :, None, :] & (rank[:, :, None, :] == slots[:, None])
    lists = jnp.sum(jnp.where(here, slots, 0), axis=3)
    return jnp.sum(jnp.where(seen, 1, 0), axis=2).astype(jnp.int32), lists.astype(jnp.int32)


def on_device(chips, mems, queries, suffix_kv, prefix_kv, out_weight, node_blocks, root_of, mid_of):
    group = lax.axis_index("grp")
    mem = lax.axis_index("mem")
    core = group % CORES
    tokens_dev, heads_dev, head_dim = queries.shape
    reqs = tokens_dev // SUFFIX
    heads = heads_dev // CORES
    per_kv = QH // KVH
    own = prefix_kv.shape[0]
    half = chips // 2
    if chips == 8:
        ring = [0, 2, 4, 6, 7, 5, 3, 1]
    else:
        ring = list(range(half)) + list(range(half, chips))[::-1]

    swap = [(2 * s + c, 2 * s + 1 - c) for s in range(chips) for c in range(CORES)]
    ahead = [
        (2 * ring[i] + c, 2 * ring[(i + 1) % chips] + c) for i in range(chips) for c in range(CORES)
    ]
    behind = [(b, a) for a, b in ahead]

    kv_start = mem * heads_dev // per_kv
    kv_count = max(1, heads_dev // per_kv)

    def of_core(heads_kv, c):
        if kv_count == 1:
            return heads_kv[0]
        return jnp.where(c == 0, heads_kv[0], heads_kv[1])

    served = lax.dynamic_slice_in_dim(prefix_kv, kv_start, kv_count, 3)
    served = jnp.transpose(served, (3, 0, 1, 2, 4))
    own_a = of_core(served, core)
    own_b = lax.ppermute(of_core(served, 1 - core), "grp", swap)

    own_b, queries, suffix_kv, node_blocks, group = lax.optimization_barrier(
        (own_b, queries, suffix_kv, node_blocks, group)
    )

    order = (jnp.arange(reqs) + mem + 1) % reqs if mems == 2 else jnp.arange(reqs)

    def ordered(x):
        x = x.reshape((reqs, SUFFIX) + x.shape[1:])
        if mems != 2:
            return x
        return jnp.where(mem == 0, x[::-1], x)

    def query_part(c):
        return lax.dynamic_slice_in_dim(q_ordered, c * heads, heads, 1)

    q_ordered = jnp.transpose(ordered(queries), (0, 2, 1, 3))
    q = [query_part(core), lax.ppermute(query_part(1 - core), "grp", swap)]
    served = lax.dynamic_slice_in_dim(suffix_kv, kv_start, kv_count, 2)
    served = jnp.transpose(ordered(served), (3, 0, 2, 1, 4))
    suffix = [of_core(served, core), lax.ppermute(of_core(served, 1 - core), "grp", swap)]

    both = jnp.stack([group, group ^ 1])
    request_ids = (both[None, :] * reqs + order[:, None]).reshape(-1)
    lo, hi = path_ranges(request_ids, node_blocks, root_of, mid_of)
    far = chips // 2
    near = [[(-k, 0), (-k, 1), (k, 0), (k, 1)] for k in range(1, far)]
    final_plan = [(-far, 0), (far, 1)]
    plan = [[(0, 0), (0, 1)]] + near + [final_plan]
    budgets = {far - 2: 30, far - 1: 22}
    work = work_tables(plan, budgets, chips, own, group, lo, hi)

    def tied(x, y, state):
        return lax.optimization_barrier((x, y, state))

    state = stage(0, work, q, None, [], suffix=suffix)
    forth, back = [own_a, own_b], [own_a, own_b]
    for k in range(1, far):
        forth = [lax.ppermute(x, "grp", ahead) for x in forth]
        back = [lax.ppermute(x, "grp", behind) for x in back]
        if k == 1:
            forth[0], back[0], state = tied(forth[0], back[0], state)
            state = stage(0, work, q, state, [own_a, own_b])
        else:
            forth[0], back[0], state = tied(forth[0], back[0], state)
            state = stage(k - 1, work, q, state, last_step)
            before_last = last_step
        forth[1], back[1], state = tied(forth[1], back[1], state)
        last_step = forth + back
    step = forth + back
    state = stage(far - 1, work, q, state, step)
    final = [lax.ppermute(forth[0], "grp", ahead), lax.ppermute(back[1], "grp", behind)]

    def attended(part, state):
        number, pieces = (far, final) if part == 0 else (far + 1, before_last + step + final)
        staying, leaving = stage(
            number, work, q, state, pieces, base=2 * part, nreq=2, last=True
        )
        return staying, lax.ppermute(leaving, "grp", swap)

    if mems != 2:
        rows = [project(core, *attended(k, state), out_weight) for k in range(reqs)]
        return lax.psum_scatter(
            jnp.concatenate(rows, axis=0), "mem", scatter_dimension=0, tiled=True
        )

    def exchange(x):
        return lax.ppermute(x, "mem", [(0, 1), (1, 0)])

    columns = out_weight.shape[1]
    split = columns // 4

    def follows(work_now, *now):
        shapes = jax.eval_shape(work_now, *now)
        return lax.cond(
            node_blocks[0] >= 0,
            work_now,
            lambda *_: jax.tree.map(lambda x: jnp.zeros(x.shape, x.dtype), shapes),
            *now,
        )

    def keep(state):
        return project(core, *attended(1, state), out_weight)

    def second(rows, state):
        sent, state = lax.optimization_barrier(
            (project(core, *rows, out_weight, split, columns - split), state)
        )
        got = exchange(sent)
        kept = follows(keep, state)
        return got, kept

    rows = attended(0, state)
    sent, rows, state = lax.optimization_barrier(
        (project(core, *rows, out_weight, 0, split), rows, state)
    )
    early = exchange(sent)
    late, kept = follows(second, rows, state)
    return add(kept, early, late)


def solution(mesh):
    return jax.shard_map(
        functools.partial(on_device, mesh.shape["grp"] // CORES, mesh.shape["mem"]),
        mesh=mesh,
        in_specs=(
            P("grp", "mem", None),
            P("grp", None, None, None),
            P("grp", None, None, None, None),
            P("mem", None),
            P(),
            P(),
            P(),
        ),
        out_specs=P(("grp", "mem"), None),
        check_vma=False,
    )
```

```python
import functools

import jax
import jax.numpy as jnp
from jax import lax
from jax.experimental import pallas as pl
from jax.experimental.pallas import tpu as pltpu
from jax.sharding import PartitionSpec as P

QH = 32
KVH = 4
SUFFIX = 256
CORES = 2
NEG = -1e30


def path_ranges(request_ids, node_blocks, root_of, mid_of):
    nodes_all = node_blocks.shape[0]
    middles_all = root_of.shape[0]
    leaves = mid_of.shape[0]
    roots_all = nodes_all - middles_all - leaves
    firsts = jnp.cumsum(node_blocks) - node_blocks
    middles = jnp.sum(
        jnp.where(jnp.arange(leaves)[None, :] == request_ids[:, None], mid_of[None, :], 0), axis=1
    )
    root_ids = jnp.sum(
        jnp.where(jnp.arange(middles_all)[None, :] == middles[:, None], root_of[None, :], 0), axis=1
    )
    path_nodes = jnp.stack(
        [root_ids, roots_all + middles, roots_all + middles_all + request_ids], axis=1
    )
    picked = jnp.arange(nodes_all)[None, None, :] == path_nodes[:, :, None]
    lower_end = jnp.sum(jnp.where(picked, firsts[None, None, :], 0), axis=2)
    upper_end = lower_end + jnp.sum(jnp.where(picked, node_blocks[None, None, :], 0), axis=2)
    return (lower_end, upper_end)


def stage_kernel(n_pieces, own, number, first, last, base, *refs):
    refs = list(refs)
    count_ref, list_ref, mine_ref, theirs_ref = refs[:4]
    refs = refs[4:]
    if first:
        suffix_refs, refs = refs[:2], refs[2:]
    else:
        state_in, refs = refs[:3], refs[3:]
    pieces, refs = refs[:n_pieces], refs[n_pieces:]
    if last:
        out_refs, state_refs, refs = refs[:2], refs[2:5], refs[5:]
        m_ref, l_ref, acc_ref = state_refs
    else:
        m_ref, l_ref, acc_ref = refs[:3]
        refs = refs[3:]
    kv_ref, q_ref, piece_sems, q_sems = refs
    nreq, heads, rows, head_dim = q_ref.shape
    scale = head_dim ** (-0.5)
    first_row = 0 if last else base

    def q_copy(j):
        source = (mine_ref, theirs_ref)[(base + j) % 2].at[(base + j) // 2]
        return pltpu.make_async_copy(source, q_ref.at[j], q_sems.at[j])

    def piece_copy(i):
        return pltpu.make_async_copy(
            pieces[i], kv_ref.at[pl.ds(i * own, own)], piece_sems.at[i]
        )

    def active(j):
        return count_ref[number, base + j] > 0

    if first:
        for j in range(nreq):
            q_copy(j).start()
    else:
        work = active(0)
        for j in range(1, nreq):
            work = work | active(j)

        @pl.when(work)
        def _():
            for i in range(n_pieces):
                piece_copy(i).start()

        for j in range(nreq):

            @pl.when(active(j))
            def _():
                q_copy(j).start()
                if last:
                    for mine, given in zip(state_refs, state_in):
                        mine[j] = given[base + j]

    def dot(a, b):
        return jnp.dot(a, b, preferred_element_type=jnp.float32)

    def sweep(j, keys, values, old, mask=None):
        size = values.shape[0]
        values = jnp.concatenate([values.T, jnp.ones((16, size), jnp.bfloat16)], axis=0)
        scores, weights, tops, totals = {}, {}, [], []
        if old:
            highest, sums = m_ref[first_row + j], l_ref[first_row + j]
        for t in range(heads + 3):
            if t < heads:
                scores[t] = lax.dot_general(
                    keys, q_ref[j, t], (((1,), (1,)), ((), ())), preferred_element_type=jnp.float32
                )
            h = t - 3
            if h >= 0:
                p, factor = weights.pop(h)
                summed = dot(values, p)
                total = summed[head_dim : head_dim + 1]
                if old:
                    acc_ref[first_row + j, h] = acc_ref[first_row + j, h] * factor + summed[:head_dim]
                    total = sums[h : h + 1] * factor + total
                else:
                    acc_ref[first_row + j, h] = summed[:head_dim]
                totals.append(total)
            h = t - 2
            if 0 <= h < heads:
                s = scores.pop(h)
                if mask is not None:
                    s = jnp.where(mask, s, NEG)
                top = jnp.max(s, axis=0, keepdims=True)
                factor = None
                if old:
                    before = highest[h : h + 1]
                    top = jnp.maximum(before, top)
                    factor = jnp.exp((before - top) * scale)
                tops.append(top)
                p = jnp.exp((s - top).astype(jnp.bfloat16) * jnp.bfloat16(scale))
                weights[h] = (p, factor)
        m_ref[first_row + j] = jnp.concatenate(tops, axis=0)
        l_ref[first_row + j] = jnp.concatenate(totals, axis=0)

    if first:
        key_at = lax.broadcasted_iota(jnp.int32, (rows, rows), 0)
        row_at = lax.broadcasted_iota(jnp.int32, (rows, rows), 1)
        for j in range(nreq):
            q_copy(j).wait()
        for side in range(2):

            def start(k, carry, side=side):
                sfx = suffix_refs[side]
                sweep(2 * k + side, sfx[k, 0], sfx[k, 1], False, key_at <= row_at)
                return carry

            lax.fori_loop(0, nreq // 2, start, 0)

        return

    @pl.when(work)
    def _():
        for i in range(n_pieces):
            piece_copy(i).wait()

    def absorb(j, at, count):
        slots = [list_ref[number, base + j, at + u] for u in range(count)]
        keys = jnp.concatenate([kv_ref[s, 0] for s in slots], axis=0)
        values = jnp.concatenate([kv_ref[s, 1] for s in slots], axis=0)
        sweep(j, keys, values, True)

    for j in range(nreq):

        @pl.when(active(j))
        def _():
            q_copy(j).wait()

    def request(j, carry):
        count = count_ref[number, base + j]
        groups = count // 8

        def eight(i, c):
            absorb(j, 8 * i, 8)
            return c

        lax.fori_loop(0, groups, eight, 0)
        for size in (4, 2, 1):

            @pl.when((count // size) % 2 == 1)
            def _():
                absorb(j, (count // (2 * size)) * (2 * size), size)

        return carry

    lax.fori_loop(0, nreq, request, 0)

    def finish(j, row, sums, values):
        for h in range(heads):
            done = values[row, h] * (1.0 / sums[row, pl.ds(h, 1), :])
            out_refs[j % 2][:, h * head_dim : (h + 1) * head_dim] = done.astype(jnp.bfloat16).T

    if last:
        for j in range(nreq):

            @pl.when(active(j))
            def _():
                finish(j, j, l_ref, acc_ref)

            @pl.when(jnp.logical_not(active(j)))
            def _():
                finish(j, base + j, state_in[1], state_in[2])


SHORT = pl.CostEstimate(flops=1, bytes_accessed=1, transcendentals=0)
SCOPED = 28 * 1024 * 1024
SMEM = pl.BlockSpec(memory_space=pltpu.SMEM)
VMEM = pl.BlockSpec(memory_space=pltpu.VMEM)
ANY = pl.BlockSpec(memory_space=pl.ANY)


def stage(number, work, queries, state, pieces, suffix=None, base=0, nreq=None, last=False):
    counts, lists = work
    half, heads, rows, head_dim = queries[0].shape
    own, _, block_tokens, _ = pieces[0].shape if pieces else (1, 2, 8, head_dim)
    first = suffix is not None
    nreq = nreq or 2 * half
    held = [
        pltpu.VMEM((nreq, heads, rows), jnp.float32),
        pltpu.VMEM((nreq, heads, rows), jnp.float32),
        pltpu.VMEM((nreq, heads, head_dim, rows), jnp.float32),
    ]
    scratch = (held if last else []) + [
        pltpu.VMEM((max(1, len(pieces)) * own, 2, block_tokens, head_dim), jnp.bfloat16),
        pltpu.VMEM((nreq, heads, rows, head_dim), jnp.bfloat16),
        pltpu.SemaphoreType.DMA((max(1, len(pieces)),)),
        pltpu.SemaphoreType.DMA((nreq,)),
    ]
    stats = jax.ShapeDtypeStruct((2 * half, heads, rows), jnp.float32)
    total = jax.ShapeDtypeStruct((2 * half, heads, head_dim, rows), jnp.float32)
    done = jax.ShapeDtypeStruct((rows, heads * head_dim), jnp.bfloat16)
    extra = suffix if first else state
    return pl.pallas_call(
        functools.partial(stage_kernel, len(pieces), own, number, first, last, base),
        in_specs=[SMEM, SMEM, ANY, ANY] + [VMEM] * len(extra) + [ANY] * len(pieces),
        out_specs=[VMEM] * 2 if last else [VMEM] * 3,
        out_shape=[done] * 2 if last else [stats, stats, total],
        scratch_shapes=scratch,
        compiler_params=pltpu.CompilerParams(vmem_limit_bytes=SCOPED),
        cost_estimate=SHORT,
        input_output_aliases={} if first or last else {4: 0, 5: 1, 6: 2},
    )(counts, lists, *queries, *extra, *pieces)


def project_kernel(start, core_ref, mine_ref, theirs_ref, weight_ref, out_ref):
    depth = mine_ref.shape[1]
    core = core_ref[0]
    columns = out_ref.shape[1]
    width = min(512, columns)
    for at in range(0, columns, width):
        across = pl.ds(start + at, width)
        summed = jnp.dot(
            mine_ref[...],
            weight_ref[pl.ds(core * depth, depth), across],
            preferred_element_type=jnp.float32,
        ) + jnp.dot(
            theirs_ref[...],
            weight_ref[pl.ds((1 - core) * depth, depth), across],
            preferred_element_type=jnp.float32,
        )
        out_ref[:, at : at + width] = summed.astype(out_ref.dtype)


def project(core, mine, theirs, out_weight, start=0, columns=None):
    columns = columns or out_weight.shape[1]
    return pl.pallas_call(
        functools.partial(project_kernel, start),
        in_specs=[SMEM, VMEM, VMEM, VMEM],
        out_specs=VMEM,
        out_shape=jax.ShapeDtypeStruct((mine.shape[0], columns), jnp.bfloat16),
        compiler_params=pltpu.CompilerParams(vmem_limit_bytes=SCOPED),
        cost_estimate=SHORT,
    )(core.reshape(1), mine, theirs, out_weight)


def add_kernel(kept_ref, *refs):
    *got_refs, out_ref = refs
    at = 0
    for got in got_refs:
        part = slice(at, at + got.shape[1])
        summed = kept_ref[:, part].astype(jnp.float32) + got[...].astype(jnp.float32)
        out_ref[:, part] = summed.astype(out_ref.dtype)
        at += got.shape[1]


def add(kept, *got):
    return pl.pallas_call(
        add_kernel,
        in_specs=[VMEM] * (1 + len(got)),
        out_specs=VMEM,
        out_shape=jax.ShapeDtypeStruct(kept.shape, jnp.bfloat16),
        compiler_params=pltpu.CompilerParams(vmem_limit_bytes=SCOPED),
        cost_estimate=SHORT,
    )(kept, *got)


def ring_order(chips, at):
    half = chips // 2
    if chips == 8:
        place = jnp.where(at % 2 == 0, at // 2, chips - 1 - at // 2)
        chip = jnp.where(at < half, 2 * at, 2 * (chips - 1 - at) + 1)
    else:
        place = jnp.where(at < half, at, chips + half - 1 - at)
        chip = place
    return place, chip


def work_tables(plan, budgets, chips, own, group, lo, hi):
    most = max(len(pieces) for pieces in plan)
    filled = [pieces + [(0, -1)] * (most - len(pieces)) for pieces in plan]
    steps = jnp.asarray([[step for step, _ in pieces] for pieces in filled], jnp.int32)
    sides = jnp.asarray([[side for _, side in pieces] for pieces in filled], jnp.int32)
    place = ring_order(chips, group // CORES)[0]
    source = ring_order(chips, (place + steps + chips) % chips)[1]
    device = jnp.where(sides < 0, -chips * CORES, CORES * source + ((group % CORES) ^ sides))
    slots = jnp.arange(most * own)
    blocks = jnp.repeat(device * own, own, axis=1) + (slots % own)[None, :]
    inside = (blocks[:, None, None, :] >= lo[None, :, :, None]) & (
        blocks[:, None, None, :] < hi[None, :, :, None]
    )
    seen = jnp.any(inside, axis=2)
    number = jnp.sum(jnp.where(seen, 1, 0), axis=2)
    nreq = lo.shape[0]
    limit = jnp.asarray([budgets.get(i, 1 << 20) for i in range(len(plan))], jnp.int32)
    load, taken = 0, []
    for j in range(nreq):
        room = number[:, j] if j < nreq // 2 else jnp.clip(limit - load, 0, number[:, j])
        load = load + room
        taken.append(room)
    before = slots[None, :] < slots[:, None]
    rank = jnp.sum(jnp.where(seen[:, :, None, :] & before, 1, 0), axis=3)
    now = rank < jnp.stack(taken, axis=1)[:, :, None]
    left = jnp.concatenate(
        [(seen & ~now)[i] for i in sorted(budgets)] + [seen[-1, :, : len(plan[-1]) * own]], axis=1
    )
    size = left.shape[1]
    seen = jnp.pad(seen & now, ((0, 0), (0, 0), (0, size - most * own)))
    seen = jnp.concatenate([seen, left[None]], axis=0)
    slots = jnp.arange(size)
    ahead = slots[None, :] < slots[:, None]
    rank = jnp.sum(jnp.where(seen[:, :, None, :] & ahead, 1, 0), axis=3)
    here = seen[:, :, None, :] & (rank[:, :, None, :] == slots[:, None])
    lists = jnp.sum(jnp.where(here, slots, 0), axis=3)
    return jnp.sum(jnp.where(seen, 1, 0), axis=2).astype(jnp.int32), lists.astype(jnp.int32)


def on_device(chips, mems, queries, suffix_kv, prefix_kv, out_weight, node_blocks, root_of, mid_of):
    group = lax.axis_index("grp")
    mem = lax.axis_index("mem")
    core = group % CORES
    tokens_dev, heads_dev, head_dim = queries.shape
    reqs = tokens_dev // SUFFIX
    heads = heads_dev // CORES
    per_kv = QH // KVH
    own = prefix_kv.shape[0]
    half = chips // 2
    if chips == 8:
        ring = [0, 2, 4, 6, 7, 5, 3, 1]
    else:
        ring = list(range(half)) + list(range(half, chips))[::-1]

    swap = [(2 * s + c, 2 * s + 1 - c) for s in range(chips) for c in range(CORES)]
    ahead = [
        (2 * ring[i] + c, 2 * ring[(i + 1) % chips] + c) for i in range(chips) for c in range(CORES)
    ]
    behind = [(b, a) for a, b in ahead]

    kv_start = mem * heads_dev // per_kv
    kv_count = max(1, heads_dev // per_kv)

    def of_core(heads_kv, c):
        if kv_count == 1:
            return heads_kv[0]
        return jnp.where(c == 0, heads_kv[0], heads_kv[1])

    served = lax.dynamic_slice_in_dim(prefix_kv, kv_start, kv_count, 3)
    served = jnp.transpose(served, (3, 0, 1, 2, 4))
    own_a, served = lax.optimization_barrier((of_core(served, core), served))
    own_b = lax.ppermute(of_core(served, 1 - core), "grp", swap)

    own_b, queries, suffix_kv, node_blocks, group = lax.optimization_barrier(
        (own_b, queries, suffix_kv, node_blocks, group)
    )

    order = (jnp.arange(reqs) + mem + 1) % reqs if mems == 2 else jnp.arange(reqs)

    def ordered(x):
        x = x.reshape((reqs, SUFFIX) + x.shape[1:])
        if mems != 2:
            return x
        return jnp.where(mem == 0, x[::-1], x)

    def query_part(c):
        return lax.dynamic_slice_in_dim(q_ordered, c * heads, heads, 1)

    q_ordered = jnp.transpose(ordered(queries), (0, 2, 1, 3))
    q = [query_part(core), lax.ppermute(query_part(1 - core), "grp", swap)]
    served = lax.dynamic_slice_in_dim(suffix_kv, kv_start, kv_count, 2)
    served = jnp.transpose(ordered(served), (3, 0, 2, 1, 4))
    suffix = [of_core(served, core), lax.ppermute(of_core(served, 1 - core), "grp", swap)]

    both = jnp.stack([group, group ^ 1])
    request_ids = (both[None, :] * reqs + order[:, None]).reshape(-1)
    lo, hi = path_ranges(request_ids, node_blocks, root_of, mid_of)
    far = chips // 2
    near = [[(-k, 0), (-k, 1), (k, 0), (k, 1)] for k in range(1, far)]
    final_plan = [(-far, 0), (far, 1)]
    plan = [[(0, 0), (0, 1)]] + near + [final_plan]
    budgets = {far - 2: 30, far - 1: 22}
    work = work_tables(plan, budgets, chips, own, group, lo, hi)

    def tied(x, y, state):
        return lax.optimization_barrier((x, y, state))

    state = stage(0, work, q, None, [], suffix=suffix)
    forth, back = [own_a, own_b], [own_a, own_b]
    for k in range(1, far):
        forth = [lax.ppermute(x, "grp", ahead) for x in forth]
        back = [lax.ppermute(x, "grp", behind) for x in back]
        if k == 1:
            forth[0], back[0], state = tied(forth[0], back[0], state)
            state = stage(0, work, q, state, [own_a, own_b])
        else:
            forth[0], back[0], state = tied(forth[0], back[0], state)
            state = stage(k - 1, work, q, state, last_step)
            before_last = last_step
        forth[1], back[1], state = tied(forth[1], back[1], state)
        last_step = forth + back
    step = forth + back
    state = stage(far - 1, work, q, state, step)
    final = [lax.ppermute(forth[0], "grp", ahead), lax.ppermute(back[1], "grp", behind)]

    def attended(part, state):
        number, pieces = (far, final) if part == 0 else (far + 1, before_last + step + final)
        staying, leaving = stage(
            number, work, q, state, pieces, base=2 * part, nreq=2, last=True
        )
        return staying, lax.ppermute(leaving, "grp", swap)

    if mems != 2:
        rows = [project(core, *attended(k, state), out_weight) for k in range(reqs)]
        return lax.psum_scatter(
            jnp.concatenate(rows, axis=0), "mem", scatter_dimension=0, tiled=True
        )

    def exchange(x):
        return lax.ppermute(x, "mem", [(0, 1), (1, 0)])

    columns = out_weight.shape[1]
    split = columns // 4

    def follows(work_now, *now):
        shapes = jax.eval_shape(work_now, *now)
        return lax.cond(
            node_blocks[0] >= 0,
            work_now,
            lambda *_: jax.tree.map(lambda x: jnp.zeros(x.shape, x.dtype), shapes),
            *now,
        )

    def keep(state):
        return project(core, *attended(1, state), out_weight)

    def second(rows, state):
        sent, state = lax.optimization_barrier(
            (project(core, *rows, out_weight, split, columns - split), state)
        )
        got = exchange(sent)
        kept = follows(keep, state)
        return got, kept

    rows = attended(0, state)
    sent, rows, state = lax.optimization_barrier(
        (project(core, *rows, out_weight, 0, split), rows, state)
    )
    early = exchange(sent)
    late, kept = follows(second, rows, state)
    return add(kept, early, late)


def solution(mesh):
    return jax.shard_map(
        functools.partial(on_device, mesh.shape["grp"] // CORES, mesh.shape["mem"]),
        mesh=mesh,
        in_specs=(
            P("grp", "mem", None),
            P("grp", None, None, None),
            P("grp", None, None, None, None),
            P("mem", None),
            P(),
            P(),
            P(),
        ),
        out_specs=P(("grp", "mem"), None),
        check_vma=False,
    )
```
